128 devices in a mesh: seq: 32 (over z, y, core), grp: 4 (over x).
Axes of the slice: x: 4, y: 4, z: 4, core: 2. Of those that a mesh axis runs over, the one named last changes fastest.
Arguments:
- query_states: bfloat16 [64, 16384, 128], P('grp', 'seq'), may hold values from -6 to 6
- key_states: bfloat16 [8, 16384, 128], P('grp', 'seq'), may hold values from -6 to 6
- value_states: bfloat16 [8, 16384, 128], P('grp', 'seq'), may hold values from -6 to 6
- tile_keys: int32 [64, 128, 16], P('grp'), may hold values from 0 to 127, as said below
- tile_count: int32 [64, 128], P('grp'), may hold values from 1 to 16, as said below
- out_weight: bfloat16 [8192, 4096], P('grp'), may hold values from -0.0625 to 0.0625
Outputs:
- projected: bfloat16 [16384, 4096], P(('seq', 'grp'))
The draws below stay inside these ranges and needn't reach their ends.
Inputs may be any that keep to these rules, and one draw needn't show every extreme that they name: `tile_count`: for each head and query block, at least one and at most 16 key blocks are named; 16 is reached. `tile_keys`: for head h and query block i, slots 0 to tile_count[h, i] - 1 name distinct key blocks in falling order, the first being block i itself and none after i; the remaining slots hold 0.
All inputs are finite; a program needn't handle non-finite values.
Results may differ from the reference program's by a relative error of at most 0.0056.
Values may be sent and summed in bfloat16 or wider, within the bound.
No kernel may reach another device: no remote copies, remote signals or barrier semaphores. Data moves between devices by JAX's collectives and lax.ppermute only.
A program may use at most 128 MiB of HBM per device.

```python
import jax
import jax.numpy as jnp
from jax import lax

HEADS = 64
KVH = 8
HD = 128
DWIN = 4096
BLK = 128
MAXT = 16
SEQ = 16384
QB = 128


def tile_pattern(key):
    key = jax.random.fold_in(key, 101)
    streams = jax.random.split(key, 5)
    slash_level = jax.random.randint(streams[0], (HEADS,), 4, 72)
    vertical_level = jax.random.randint(streams[1], (HEADS,), 2, 40)
    slash_draws = jax.random.randint(streams[2], (HEADS, QB), 0, 256)
    vertical_draws = jax.random.randint(streams[3], (HEADS, QB), 0, 256)
    heavy_head = jax.random.randint(streams[4], (), 0, HEADS)
    offsets = jnp.arange(QB, dtype=jnp.int32)
    head_index = jnp.arange(HEADS, dtype=jnp.int32)
    slash_on = (slash_draws < slash_level[:, None]) | (head_index[:, None] == heavy_head) & (offsets[None, :] < MAXT)
    vertical_on = (vertical_draws < vertical_level[:, None]) | (offsets[None, :] == 0)
    distance = offsets[:, None] - offsets[None, :]
    slash_hit = jnp.take(slash_on, jnp.clip(distance, 0, QB - 1), axis=1)
    named = (distance >= 0)[None, :, :] & ((distance == 0)[None, :, :] | slash_hit | vertical_on[:, None, :])
    ranking = jnp.where(named, QB + offsets[None, None, :], -1 - offsets[None, None, :])
    chosen = lax.top_k(ranking, MAXT)[0]
    lists = jnp.where(chosen >= QB, chosen - QB, 0).astype(jnp.int32)
    counts = jnp.minimum(jnp.sum(named.astype(jnp.int32), axis=-1), MAXT).astype(jnp.int32)
    return (lists, counts)


def draw_tile_keys(key, part):
    lists, counts = tile_pattern(key)
    return lists


def draw_tile_count(key, part):
    lists, counts = tile_pattern(key)
    return counts


def draw_query_states(key, part):
    key = jax.random.fold_in(key, 3)
    base = jnp.clip(jax.random.normal(key, (HEADS, SEQ, HD), jnp.float32), -6.0, 6.0)
    return base.astype(jnp.bfloat16)


def draw_key_states(key, part):
    key = jax.random.fold_in(key, 5)
    base = jnp.clip(jax.random.normal(key, (KVH, SEQ, HD), jnp.float32), -6.0, 6.0)
    return base.astype(jnp.bfloat16)


def shard_levels(own_key, dims, pieces, smallest, top_value):
    def one(axis_at, blocks):
        draws = jax.random.uniform(jax.random.fold_in(jax.random.fold_in(own_key, 6), axis_at), (blocks,), jnp.float32, smallest / len(pieces), top_value / len(pieces))
        return jnp.repeat(jnp.exp(draws), dims[axis_at] // blocks).reshape((-1,) + (1,) * (len(dims) - axis_at - 1))

    level = one(*pieces[0])
    for cut in pieces[1:]:
        level = level * one(*cut)
    return level


def gaussian(key, shape, spread, bound, cuts=(), kind=jnp.bfloat16):
    drawn = spread * jax.random.normal(key, shape, jnp.float32)
    if cuts:
        drawn = drawn * shard_levels(key, shape, cuts, -0.22, 0.18)
    return jnp.clip(drawn, -bound, bound).astype(kind)


def setup_inputs(seed: int = 0) -> dict:
    key_of = jax.random.split(jax.random.key(seed), 7)
    return {
        "query_states": draw_query_states(jax.random.fold_in(key_of[6], 71), 0),
        "key_states": draw_key_states(jax.random.fold_in(key_of[6], 71), 0),
        "value_states": gaussian(key_of[2], (KVH, SEQ, HD), 1.0, 6.0, ((0, 4), (1, 32))),
        "tile_keys": draw_tile_keys(jax.random.fold_in(key_of[6], 71), 0),
        "tile_count": draw_tile_count(jax.random.fold_in(key_of[6], 71), 0),
        "out_weight": gaussian(key_of[5], (HEADS * HD, DWIN), (HEADS * HD) ** -0.5, 0.0625, ((0, 4),)),
    }


def allowed_mask(used_slots, count_batch, block_batch, block_rows):
    slot_span = used_slots.shape[1]
    column = jnp.arange(slot_span * block_rows, dtype=jnp.int32)
    slot_of = column // block_rows
    inner_pos = column % block_rows
    key_block = used_slots[:, slot_of]
    live_slot = slot_of[None, :] < count_batch[:, None]
    own_block = key_block == block_batch[:, None]
    row_index = jnp.arange(block_rows, dtype=jnp.int32)
    earlier = inner_pos[None, :] <= row_index[:, None]
    return live_slot[:, None, :] & (jnp.logical_not(own_block)[:, None, :] | earlier[None, :, :])


def block_attention(query_batch, list_batch, count_batch, block_batch, key_head, value_head):
    batch_size, block_rows, head_width = query_batch.shape
    slot_span = list_batch.shape[1]
    key_tiles = key_head[list_batch].reshape(batch_size, slot_span * block_rows, head_width).astype(jnp.float32)
    value_tiles = value_head[list_batch].reshape(batch_size, slot_span * block_rows, head_width).astype(jnp.float32)
    scores = jnp.einsum("gqd,gkd->gqk", query_batch.astype(jnp.float32), key_tiles,
                        precision=lax.Precision.HIGHEST) * (HD ** -0.5)
    allowed = allowed_mask(list_batch, count_batch, block_batch, block_rows)
    scores = jnp.where(allowed, scores, -jnp.inf)
    row_top = jnp.max(scores, axis=-1, keepdims=True)
    weights = jnp.exp(scores - row_top)
    row_total = jnp.sum(weights, axis=-1, keepdims=True)
    rounded = lax.optimization_barrier(weights.astype(jnp.bfloat16)).astype(jnp.float32)
    summed = jnp.einsum("gqk,gkd->gqd", rounded, value_tiles, precision=lax.Precision.HIGHEST)
    return (summed / row_total).astype(jnp.bfloat16)


def reference(query_states, key_states, value_states, tile_keys, tile_count, out_weight):
    query_blocks = query_states.reshape(HEADS, QB, BLK, HD)
    key_blocks = key_states.reshape(KVH, QB, BLK, HD)
    value_blocks = value_states.reshape(KVH, QB, BLK, HD)
    head_ratio = HEADS // KVH
    batch_total = QB // 8

    def one_head(head_index):
        head_queries = query_blocks[head_index].reshape(batch_total, 8, BLK, HD)
        key_head = key_blocks[head_index // head_ratio]
        value_head = value_blocks[head_index // head_ratio]
        head_lists = tile_keys[head_index].reshape(batch_total, 8, MAXT)
        head_counts = tile_count[head_index].reshape(batch_total, 8)
        block_ids = jnp.arange(QB, dtype=jnp.int32).reshape(batch_total, 8)

        def one_batch(packed):
            query_batch, list_batch, count_batch, block_batch = packed
            return block_attention(query_batch, list_batch, count_batch, block_batch, key_head, value_head)

        result = lax.map(one_batch, (head_queries, head_lists, head_counts, block_ids))
        return result.reshape(SEQ, HD)

    attended = lax.map(one_head, jnp.arange(HEADS, dtype=jnp.int32))
    flat_rows = attended.transpose(1, 0, 2).reshape(SEQ, HEADS * HD)
    return jnp.dot(flat_rows, out_weight, preferred_element_type=jnp.float32).astype(jnp.bfloat16)
```

```python
import math

import jax
import jax.numpy as jnp
from jax import lax
from jax.experimental import pallas as pl
from jax.experimental.pallas import tpu as pltpu
from jax.sharding import PartitionSpec as P

BLK = 128
SLOTS = 16
EXP2_SCALE = float(BLK ** -0.5 * math.log2(math.e))
LOW = -1e30


def attention_kernel(head_count, block_count, kv_ratio, lists, counts, q_ref, table_ref, out_ref, score_a, score_b, top_a, top_b):
    couples_per_block = head_count // 2
    couple_total = couples_per_block * block_count
    lanes = 2 * BLK
    key_row = lax.broadcasted_iota(jnp.int32, (BLK, lanes), 0)
    query_row = lax.broadcasted_iota(jnp.int32, (BLK, lanes), 1) % BLK
    lane = lax.broadcasted_iota(jnp.int32, (1, lanes), 1)
    zero = jnp.zeros((BLK, BLK), jnp.bfloat16)

    def place(couple):
        return couple // couples_per_block, 2 * (couple % couples_per_block)

    def pair_ids(couple):
        block, head = place(couple)
        return head * block_count + block, (head + 1) * block_count + block

    def live(couple):
        a, b = pair_ids(couple)
        return jnp.where(lane < BLK, counts[a], counts[b])

    def score_all(couple, score_ref, top_ref):
        block, head = place(couple)
        a, b = pair_ids(couple)
        rows = pl.ds(pl.multiple_of(block * BLK, BLK), BLK)
        qa = q_ref[head, rows, :].T
        qb = q_ref[head + 1, rows, :].T
        queries = jnp.concatenate(
            [jnp.concatenate([qa, zero], 1), jnp.concatenate([zero, qb], 1)], 0
        )
        keys = jnp.concatenate(
            [
                jnp.concatenate(
                    [table_ref[lists[a * SLOTS + n]], table_ref[lists[b * SLOTS + n]]], 1
                )
                for n in range(SLOTS)
            ],
            0,
        )
        scores = jnp.dot(keys, queries, preferred_element_type=jnp.float32)
        count = live(couple)
        top = None
        for n in range(SLOTS):
            tile = scores[n * BLK : (n + 1) * BLK]
            if n == 0:
                tile = jnp.where(key_row <= query_row, tile, LOW)
                top = tile.reshape(16, 8, lanes).max(0)
            else:
                best = tile.reshape(16, 8, lanes).max(0)
                top = jnp.maximum(top, jnp.where(n < count, best, LOW))
            score_ref[n * BLK : (n + 1) * BLK, :] = tile
        top_ref[...] = jnp.max(top, axis=0, keepdims=True)

    def weigh_all(couple, score_ref, top_ref, value_step):
        block, head = place(couple)
        a, b = pair_ids(couple)
        count = live(couple)
        top = top_ref[...]
        total = jnp.zeros((8, lanes), jnp.float32)
        parts = []
        for n in range(SLOTS):
            shift = top if n == 0 else jnp.where(n < count, top, -LOW)
            weights = jnp.exp2((score_ref[n * BLK : (n + 1) * BLK, :] - shift) * EXP2_SCALE)
            total += weights.reshape(16, 8, lanes).sum(0)
            parts.append(weights.astype(jnp.bfloat16))
        rounded = jnp.concatenate(parts, 0)
        row_total = jnp.sum(total, axis=0, keepdims=True)
        rows = pl.ds(pl.multiple_of(block * BLK, BLK), BLK)
        for side, pair in enumerate((a, b)):
            values = jnp.concatenate(
                [table_ref[lists[pair * SLOTS + n] + value_step] for n in range(SLOTS)], 1
            )
            mine = slice(side * BLK, (side + 1) * BLK)
            summed = jnp.dot(values, rounded[:, mine], preferred_element_type=jnp.float32)
            attended = (summed / row_total[:, mine]).T.astype(jnp.bfloat16)
            cols = pl.ds(pl.multiple_of((head + side) * BLK, BLK), BLK)
            out_ref[rows, cols] = attended

    value_step = kv_ratio
    score_all(0, score_a, top_a)

    def step(index, carry):
        first = 2 * index
        score_all(first + 1, score_b, top_b)
        weigh_all(first, score_a, top_a, value_step)
        score_all(jnp.minimum(first + 2, couple_total - 1), score_a, top_a)
        weigh_all(first + 1, score_b, top_b, value_step)
        return carry

    lax.fori_loop(0, couple_total // 2, step, 0)


def attend(lists, counts, queries, table, value_step):
    head_count, rows, width = queries.shape
    block_count = rows // BLK

    def kernel(*refs):
        attention_kernel(head_count, block_count, value_step, *refs)

    whole = pl.BlockSpec(memory_space=pltpu.VMEM)
    return pl.pallas_call(
        kernel,
        name="attend",
        grid_spec=pltpu.PrefetchScalarGridSpec(
            num_scalar_prefetch=2,
            grid=(1,),
            in_specs=[whole, whole],
            out_specs=whole,
            scratch_shapes=[pltpu.VMEM((SLOTS * BLK, 2 * BLK), jnp.float32)] * 2
            + [pltpu.VMEM((1, 2 * BLK), jnp.float32)] * 2,
        ),
        out_shape=jax.ShapeDtypeStruct((rows, head_count * width), jnp.bfloat16),
        compiler_params=pltpu.CompilerParams(vmem_limit_bytes=56 * 2**20),
    )(lists, counts, queries, table)


def body(query_states, key_states, value_states, tile_keys, tile_count, out_weight):
    head_group, row_count, width = query_states.shape
    kv_group = key_states.shape[0]
    blocks = row_count // BLK
    seq_place = lax.axis_index("seq")
    key_tiles = key_states.reshape(kv_group, blocks, BLK, width)
    value_tiles = jnp.swapaxes(value_states.reshape(kv_group, blocks, BLK, width), 2, 3)
    local = jnp.stack([key_tiles, value_tiles])
    gathered = lax.all_gather(local, "seq", axis=0, tiled=False)
    table = gathered.reshape(-1, BLK, width)
    per_shard = 2 * kv_group * blocks
    lists = lax.dynamic_slice_in_dim(tile_keys, seq_place * blocks, blocks, 1)
    counts = lax.dynamic_slice_in_dim(tile_count, seq_place * blocks, blocks, 1)
    kv_of = jnp.arange(head_group, dtype=jnp.int32) // (head_group // kv_group)
    lists = (lists // blocks) * per_shard + kv_of[:, None, None] * blocks + lists % blocks
    attended = attend(
        lists.reshape(-1), counts.reshape(-1), query_states, table, kv_group * blocks
    )
    partial = jnp.dot(attended, out_weight, preferred_element_type=jnp.float32)
    return lax.psum_scatter(
        partial.astype(jnp.bfloat16), "grp", scatter_dimension=0, tiled=True
    )


def solution(mesh):
    placed = (
        P("grp", "seq", None),
        P("grp", "seq", None),
        P("grp", "seq", None),
        P("grp", None, None),
        P("grp", None),
        P("grp", None),
    )
    return jax.shard_map(
        body, mesh=mesh, in_specs=placed, out_specs=P(("seq", "grp"), None), check_vma=False
    )
```

```python
import functools
import math

import jax
import jax.numpy as jnp
from jax import lax
from jax.experimental import pallas as pl
from jax.experimental.pallas import tpu as pltpu
from jax.sharding import PartitionSpec as P

BLK = 128
SLOTS = 16
PAIR = 2 * BLK
SPAN = SLOTS * BLK
RING = 4
CORES = 2
SEQ_DEVICES = RING * RING * CORES
CHUNK_COUPLES = 8
EXP2_SCALE = float(BLK ** -0.5 * math.log2(math.e))
LOW = -1e30
LIMIT = 16 * 2**20

VMEM = pl.BlockSpec(memory_space=pltpu.VMEM)
HBM = pl.BlockSpec(memory_space=pltpu.HBM)


def cat(parts, axis):
    return jnp.concatenate(parts, axis)


def score_kernel(first, groups, lists, counts, place, q_ref, *refs):
    pieces, refs = refs[:10], refs[10:]
    weight_refs, total_ref, refs = refs[:groups], refs[groups], refs[groups + 1 :]
    score_a, score_b, top_a, top_b, table, sems = refs
    key_row = lax.broadcasted_iota(jnp.int32, (BLK, PAIR), 0)
    query_row = lax.broadcasted_iota(jnp.int32, (BLK, PAIR), 1) % BLK
    lane = lax.broadcasted_iota(jnp.int32, (1, PAIR), 1)
    zero = jnp.zeros((BLK, BLK), jnp.bfloat16)
    last = first + groups * CHUNK_COUPLES - 1

    copies, at = [], 0
    for index, piece in enumerate(pieces):
        size = piece.shape[0]
        copies.append(
            pltpu.make_async_copy(piece, table.at[pl.ds(at, size)], sems.at[index])
        )
        at += size
    for copy in copies:
        copy.start()
    for copy in copies:
        copy.wait()

    def live(couple):
        return jnp.where(lane < BLK, counts[2 * couple], counts[2 * couple + 1])

    def score(couple, score_ref, top_ref):
        chunk = couple // CHUNK_COUPLES
        side = (couple // 4) % 2
        head = 2 * (couple % 4)
        rows = pl.ds(pl.multiple_of(place[1 + chunk] * BLK, BLK), BLK)
        qa = q_ref[side, head, rows, :].T
        qb = q_ref[side, head + 1, rows, :].T
        queries = cat([cat([qa, zero], 1), cat([zero, qb], 1)], 0)
        a = 2 * couple * SLOTS
        keys = cat(
            [cat([table[lists[a + n]], table[lists[a + SLOTS + n]]], 1) for n in range(SLOTS)], 0
        )
        scores = jnp.dot(keys, queries, preferred_element_type=jnp.float32)
        count = live(couple)
        top = None
        for n in range(SLOTS):
            tile = scores[n * BLK : (n + 1) * BLK]
            if n == 0:
                tile = jnp.where(key_row <= query_row, tile, LOW)
                top = tile.reshape(16, 8, PAIR).max(0)
            else:
                best = tile.reshape(16, 8, PAIR).max(0)
                top = jnp.maximum(top, jnp.where(n < count, best, LOW))
            score_ref[n * BLK : (n + 1) * BLK, :] = tile
        top_ref[...] = jnp.max(top, axis=0, keepdims=True)

    def weigh(couple, slot, weight_ref, score_ref, top_ref):
        count = live(couple)
        top = top_ref[...]
        total = jnp.zeros((8, PAIR), jnp.float32)
        for n in range(SLOTS):
            shift = top if n == 0 else jnp.where(n < count, top, -LOW)
            weights = jnp.exp2((score_ref[n * BLK : (n + 1) * BLK, :] - shift) * EXP2_SCALE)
            total += weights.reshape(16, 8, PAIR).sum(0)
            weight_ref[slot, n * BLK : (n + 1) * BLK, :] = weights.astype(jnp.bfloat16)
        total_ref[couple - first] = jnp.sum(total, axis=0, keepdims=True)

    score(first, score_a, top_a)
    for group in range(groups):
        base = first + group * CHUNK_COUPLES

        def step(index, carry, base=base, weight_ref=weight_refs[group]):
            couple = base + 2 * index
            score(couple + 1, score_b, top_b)
            weigh(couple, 2 * index, weight_ref, score_a, top_a)
            score(jnp.minimum(couple + 2, last), score_a, top_a)
            weigh(couple + 1, 2 * index + 1, weight_ref, score_b, top_b)
            return carry

        lax.fori_loop(0, CHUNK_COUPLES // 2, step, 0)


def score_call(name, first, groups, lists, counts, place, queries, pieces):
    couples = groups * CHUNK_COUPLES
    return pl.pallas_call(
        functools.partial(score_kernel, first, groups),
        name=name,
        grid_spec=pltpu.PrefetchScalarGridSpec(
            num_scalar_prefetch=3,
            grid=(1,),
            in_specs=[VMEM] + [HBM] * len(pieces),
            out_specs=[VMEM] * (groups + 1),
            scratch_shapes=[pltpu.VMEM((SPAN, PAIR), jnp.float32)] * 2
            + [pltpu.VMEM((1, PAIR), jnp.float32)] * 2
            + [
                pltpu.VMEM((BLK, BLK, BLK), jnp.bfloat16),
                pltpu.SemaphoreType.DMA((len(pieces),)),
            ],
        ),
        out_shape=[pltpu.VMEM((CHUNK_COUPLES, SPAN, PAIR), jnp.bfloat16)] * groups
        + [jax.ShapeDtypeStruct((couples, 1, PAIR), jnp.float32)],
        compiler_params=pltpu.CompilerParams(vmem_limit_bytes=LIMIT),
        cost_estimate=pl.CostEstimate(
            flops=couples * 2 * SPAN * PAIR * PAIR,
            bytes_accessed=couples * SPAN * PAIR * 2,
            transcendentals=couples * SPAN * PAIR,
        ),
    )(lists, counts, place, queries, *pieces)


def combine(couple, slot, group, lists, weight_ref, total, values_ref, out_ref):
    head = 2 * (couple % 4)
    for side in range(2):
        pair = 2 * couple + side
        values = cat([values_ref[lists[pair * SLOTS + n]] for n in range(SLOTS)], 1)
        mine = slice(side * BLK, (side + 1) * BLK)
        summed = jnp.dot(values, weight_ref[slot, :, mine], preferred_element_type=jnp.float32)
        attended = (summed / total[:, mine]).T.astype(jnp.bfloat16)
        cols = pl.ds(pl.multiple_of((head + side) * BLK, BLK), BLK)
        rows = slice(group * BLK, (group + 1) * BLK)
        which = (couple // 4) % 2
        out_ref[which, rows, cols] = attended


def combine_loop(first, group, lists, weight_ref, total_ref, total_first, values_ref, out_ref):
    def step(index, carry):
        for k in range(4):
            slot = 4 * index + k
            couple = first + group * CHUNK_COUPLES + slot
            combine(
                couple,
                slot,
                group,
                lists,
                weight_ref,
                total_ref[couple - total_first],
                values_ref,
                out_ref,
            )
        return carry

    lax.fori_loop(0, CHUNK_COUPLES // 4, step, 0)


def first_values_kernel(lists, place, weight_ref, total_ref, gathered_ref, out_ref, values_ref, sem):
    copy = pltpu.make_async_copy(gathered_ref.at[:, place[0]], values_ref, sem)
    copy.start()
    copy.wait()
    values = values_ref.reshape(BLK, BLK, BLK)
    combine_loop(0, 0, lists, weight_ref, total_ref, 0, values, out_ref)


def first_values_call(lists, place, weights, totals, gathered):
    shards, _, tiles = gathered.shape[:3]
    return pl.pallas_call(
        first_values_kernel,
        name="values_first",
        grid_spec=pltpu.PrefetchScalarGridSpec(
            num_scalar_prefetch=2,
            grid=(1,),
            in_specs=[VMEM, VMEM, HBM],
            out_specs=[VMEM, VMEM],
            scratch_shapes=[pltpu.SemaphoreType.DMA],
        ),
        out_shape=[
            jax.ShapeDtypeStruct((2, BLK, 8 * BLK), jnp.bfloat16),
            pltpu.VMEM((shards, tiles, BLK, BLK), jnp.bfloat16),
        ],
        compiler_params=pltpu.CompilerParams(vmem_limit_bytes=LIMIT),
        cost_estimate=pl.CostEstimate(
            flops=CHUNK_COUPLES * 2 * SPAN * PAIR * BLK,
            bytes_accessed=CHUNK_COUPLES * SPAN * PAIR * 2,
            transcendentals=0,
        ),
    )(lists, place, weights, totals, gathered)


def next_values_kernel(
    first, total_first, groups, with_weight, lists, total_ref, values_ref, after_ref, *refs
):
    weight_refs, refs = refs[:groups], refs[groups:]
    if with_weight:
        proj_ref, out_ref, held_ref, sem = refs
        copy = pltpu.make_async_copy(proj_ref, held_ref, sem)
        copy.start()
    else:
        (out_ref,) = refs
    values = values_ref.reshape(BLK, BLK, BLK)
    for group in range(groups):
        combine_loop(
            first, group, lists, weight_refs[group], total_ref, total_first, values, out_ref
        )
    if with_weight:
        copy.wait()


def next_values_call(name, first, total_first, lists, totals, values, after, weights, proj=None):
    groups = len(weights)
    with_weight = proj is not None
    out_shape = [jax.ShapeDtypeStruct((2, groups * BLK, 8 * BLK), jnp.bfloat16)]
    if with_weight:
        out_shape.append(pltpu.VMEM(proj.shape, proj.dtype))
    return pl.pallas_call(
        functools.partial(next_values_kernel, first, total_first, groups, with_weight),
        name=name,
        grid_spec=pltpu.PrefetchScalarGridSpec(
            num_scalar_prefetch=1,
            grid=(1,),
            in_specs=[VMEM, VMEM, HBM] + [VMEM] * groups + [HBM] * with_weight,
            out_specs=[VMEM] * len(out_shape),
            scratch_shapes=[pltpu.SemaphoreType.DMA] * with_weight,
        ),
        out_shape=out_shape,
        compiler_params=pltpu.CompilerParams(vmem_limit_bytes=LIMIT),
        cost_estimate=pl.CostEstimate(
            flops=groups * CHUNK_COUPLES * 2 * SPAN * PAIR * BLK,
            bytes_accessed=groups * CHUNK_COUPLES * SPAN * PAIR * 2,
            transcendentals=0,
        ),
    )(lists, totals, values, after, *weights, *((proj,) if with_weight else ()))


def project_kernel(kind, place, mine_ref, theirs_ref, held_ref, *refs):
    rows = mine_ref.shape[0]
    depth = mine_ref.shape[1]
    width = held_ref.shape[1]
    tile = 1024
    core = place[0]
    mine = mine_ref[...]
    theirs = theirs_ref[...]
    left = jnp.where(core == 0, mine, theirs)
    right = jnp.where(core == 0, theirs, mine)
    both = cat([left, right], 1)
    for at in range(0, width, tile):
        cols = slice(at, at + tile)
        total = jnp.dot(both, held_ref[:, cols], preferred_element_type=jnp.float32)
        if kind == "far":
            low_ref, high_ref = refs
            if at < width // 2:
                low_ref[:, cols] = total.astype(jnp.bfloat16)
            else:
                high_ref[:, at - width // 2 : at - width // 2 + tile] = total.astype(jnp.bfloat16)
        elif kind == "near":
            low_in, high_in, up_ref, down_ref = refs
            up = total[:BLK]
            down = total[BLK:]
            if at < width // 2:
                up = up + low_in[:, cols].astype(jnp.float32)
            else:
                start = at - width // 2
                down = down + high_in[:, start : start + tile].astype(jnp.float32)
            up_ref[:, cols] = up.astype(jnp.bfloat16)
            down_ref[:, cols] = down.astype(jnp.bfloat16)
        else:
            (out_ref,) = refs
            out_ref[:, cols] = total


def project_call(kind, place, mine, theirs, held, *arrived):
    width = held.shape[1]
    shapes = {
        "far": [((BLK, width // 2), jnp.bfloat16)] * 2,
        "near": [((BLK, width), jnp.bfloat16)] * 2,
        "own": [((BLK, width), jnp.float32)],
    }[kind]
    rows = mine.shape[0]
    return pl.pallas_call(
        functools.partial(project_kernel, kind),
        name="project_" + kind,
        grid_spec=pltpu.PrefetchScalarGridSpec(
            num_scalar_prefetch=1,
            grid=(1,),
            in_specs=[VMEM] * (3 + len(arrived)),
            out_specs=[VMEM] * len(shapes),
        ),
        out_shape=[jax.ShapeDtypeStruct(*shape) for shape in shapes],
        compiler_params=pltpu.CompilerParams(vmem_limit_bytes=LIMIT),
        cost_estimate=pl.CostEstimate(
            flops=2 * rows * held.shape[0] * width,
            bytes_accessed=held.shape[0] * width * 2,
            transcendentals=0,
        ),
    )(place, mine, theirs, held, *arrived)


def chip_perm(phase, step):
    pairs = []
    for z in range(RING):
        for y in range(RING):
            for core in range(CORES):
                if (core == 0) == (phase == 0):
                    to_z, to_y = z, (y + step) % RING
                else:
                    to_z, to_y = (z + step) % RING, y
                pairs.append(((z * RING + y) * CORES + core, (to_z * RING + to_y) * CORES + core))
    return pairs


SWAP = [(i, i ^ 1) for i in range(SEQ_DEVICES)]


def along(array, phase, step):
    return lax.ppermute(array, "seq", chip_perm(phase, step))


def swap(array):
    return lax.ppermute(array, "seq", SWAP)


def turn(array, step):
    return lax.ppermute(array, "grp", [(i, (i + step) % RING) for i in range(RING)])


def gather_keys(own):
    left, right = along(own, 0, 1), along(own, 0, -1)
    far = along(own, 0, 2)
    low, high = cat([own, left], 0), cat([right, far], 0)
    left_low, right_high = along(low, 1, 1), along(high, 1, -1)
    left_high, right_low = along(high, 1, 1), along(low, 1, -1)
    far_low, far_high = along(left_low, 1, 1), along(right_high, 1, -1)
    return [own, left, right, far, left_low, left_high, right_low, right_high, far_low, far_high]


def body(query_states, key_states, value_states, tile_keys, tile_count, out_weight):
    head_group, row_count, width = query_states.shape
    kv_group = key_states.shape[0]
    blocks = row_count // BLK
    heads = head_group // kv_group
    seq_place = lax.axis_index("seq")
    grp_place = lax.axis_index("grp")
    core = seq_place % CORES
    chip = seq_place // CORES
    chip_z, chip_y = chip // RING, chip % RING

    value_tiles = jnp.swapaxes(value_states.reshape(kv_group, blocks, BLK, width), 2, 3)
    gathered = lax.all_gather(value_tiles, "seq", axis=0, tiled=False)

    key_tiles = key_states.reshape(kv_group, blocks, BLK, width)
    own_keys = cat(
        [
            lax.dynamic_index_in_dim(key_tiles, core, 0, keepdims=False),
            swap(lax.dynamic_index_in_dim(key_tiles, 1 - core, 0, keepdims=False)),
        ],
        0,
    )
    pieces = gather_keys(own_keys)

    queries = jnp.stack(
        [
            swap(lax.dynamic_slice_in_dim(query_states, (1 - core) * heads, heads, 0)),
            lax.dynamic_slice_in_dim(query_states, core * heads, heads, 0),
        ]
    )

    chunks = (grp_place + jnp.array([2, 1, 3, 0], jnp.int32)) % RING
    place = jnp.concatenate([core[None], chunks]).astype(jnp.int32)
    sides = jnp.stack([1 - core, core])
    order = (chip * 2 * blocks + sides[None, :] * blocks + chunks[:, None]).reshape(-1)
    my_lists = lax.dynamic_slice_in_dim(tile_keys, core * heads, heads, 0)
    my_counts = lax.dynamic_slice_in_dim(tile_count, core * heads, heads, 0)
    value_lists = jnp.swapaxes(jnp.take(my_lists, order, axis=1), 0, 1)
    counts = jnp.swapaxes(jnp.take(my_counts, order, axis=1), 0, 1).reshape(-1)

    span = 2 * blocks
    from_chip = value_lists // span
    inside = value_lists % span
    step_z = (from_chip // RING - chip_z) % RING
    step_y = (from_chip % RING - chip_y) % RING

    def arrival(step):
        return jnp.where(step == 1, 2, jnp.where(step == 2, 3, jnp.where(step == 3, 1, 0)))

    inner = arrival(jnp.where(core == 0, step_y, step_z))
    outer = arrival(jnp.where(core == 0, step_z, step_y))
    key_lists = (
        (outer * RING + inner) * span
        + (inside // blocks + core) % CORES * blocks
        + inside % blocks
    )
    key_lists = key_lists.reshape(-1)
    value_lists = value_lists.reshape(-1)

    far_w, up_w, down_w, totals = score_call(
        "scores", 0, 3, key_lists, counts, place, queries, pieces
    )
    far_att, values = first_values_call(value_lists, place, far_w, totals, gathered)
    near_att, held = next_values_call(
        "values_near",
        CHUNK_COUPLES,
        0,
        value_lists,
        totals,
        values,
        far_att,
        [up_w, down_w],
        out_weight,
    )
    low, high = project_call("far", place, far_att[1], swap(far_att[0]), held)
    low_in, high_in = turn(low, 1), turn(high, -1)
    own_w, own_totals = score_call(
        "scores_own", 3 * CHUNK_COUPLES, 1, key_lists, counts, place, queries, pieces
    )
    up, down = project_call(
        "near", place, near_att[1], swap(near_att[0]), held, low_in, high_in
    )
    from_left, from_right = turn(up, 1), turn(down, -1)
    (own_att,) = next_values_call(
        "values_own",
        3 * CHUNK_COUPLES,
        3 * CHUNK_COUPLES,
        value_lists,
        own_totals,
        values,
        near_att,
        [own_w],
    )
    (own,) = project_call("own", place, own_att[1], swap(own_att[0]), held)
    total = own + from_left.astype(jnp.float32) + from_right.astype(jnp.float32)
    return total.astype(jnp.bfloat16)


def solution(mesh):
    placed = (
        P("grp", "seq", None),
        P("grp", "seq", None),
        P("grp", "seq", None),
        P("grp", None, None),
        P("grp", None),
        P("grp", None),
    )
    return jax.shard_map(
        body, mesh=mesh, in_specs=placed, out_specs=P(("seq", "grp"), None), check_vma=False
    )
```

```python
import functools
import math

import jax
import jax.numpy as jnp
from jax import lax
from jax.experimental import pallas as pl
from jax.experimental.pallas import tpu as pltpu
from jax.sharding import PartitionSpec as P

BLK = 128
SLOTS = 16
PAIR = 2 * BLK
SPAN = SLOTS * BLK
RING = 4
CORES = 2
SEQ_DEVICES = RING * RING * CORES
CHUNK_COUPLES = 8
EXP2_SCALE = float(BLK ** -0.5 * math.log2(math.e))
LOW = -1e30
MIB = 2**20

SHORT = pl.CostEstimate(flops=1, bytes_accessed=1, transcendentals=0)

VMEM = pl.BlockSpec(memory_space=pltpu.VMEM)
HBM = pl.BlockSpec(memory_space=pltpu.HBM)


def stay(array):
    return pltpu.with_memory_space_constraint(array, pltpu.HBM)


def cat(parts, axis):
    return jnp.concatenate(parts, axis)


def score_couple(couple, lists, counts, place, q_ref, table, score_ref, top_ref):
    key_row = lax.broadcasted_iota(jnp.int32, (BLK, PAIR), 0)
    query_row = lax.broadcasted_iota(jnp.int32, (BLK, PAIR), 1) % BLK
    zero = jnp.zeros((BLK, BLK), jnp.bfloat16)
    chunk = couple // CHUNK_COUPLES
    side = (couple // 4) % 2
    head = 2 * (couple % 4)
    rows = pl.ds(pl.multiple_of(place[1 + chunk] * BLK, BLK), BLK)
    qa = q_ref[side, head, rows, :].T
    qb = q_ref[side, head + 1, rows, :].T
    queries = cat([cat([qa, zero], 1), cat([zero, qb], 1)], 0)
    a = 2 * couple * SLOTS
    keys = cat(
        [cat([table[lists[a + n]], table[lists[a + SLOTS + n]]], 1) for n in range(SLOTS)], 0
    )
    scores = jnp.dot(keys, queries, preferred_element_type=jnp.float32)
    count = live_counts(couple, counts)
    top = None
    for n in range(SLOTS):
        tile = scores[n * BLK : (n + 1) * BLK]
        if n == 0:
            tile = jnp.where(key_row <= query_row, tile, LOW)
            top = tile.reshape(16, 8, PAIR).max(0)
        else:
            best = tile.reshape(16, 8, PAIR).max(0)
            top = jnp.maximum(top, jnp.where(n < count, best, LOW))
        score_ref[n * BLK : (n + 1) * BLK, :] = tile
    top_ref[...] = jnp.max(top, axis=0, keepdims=True)


def live_counts(couple, counts):
    lane = lax.broadcasted_iota(jnp.int32, (1, PAIR), 1)
    return jnp.where(lane < BLK, counts[2 * couple], counts[2 * couple + 1])


def weigh_couple(couple, counts, score_ref, top_ref):
    count = live_counts(couple, counts)
    top = top_ref[...]
    total = jnp.zeros((8, PAIR), jnp.float32)
    tiles = []
    for n in range(SLOTS):
        shift = top if n == 0 else jnp.where(n < count, top, -LOW)
        weights = jnp.exp2((score_ref[n * BLK : (n + 1) * BLK, :] - shift) * EXP2_SCALE)
        total += weights.reshape(16, 8, PAIR).sum(0)
        tiles.append(weights.astype(jnp.bfloat16))
    return tiles, jnp.sum(total, axis=0, keepdims=True)


def combine_couple(couple, weights, total, lists, values, out_ref):
    side = (couple // 4) % 2
    head = 2 * (couple % 4)
    for half in range(2):
        pair = 2 * couple + half
        tiles = cat([values[lists[pair * SLOTS + n]] for n in range(SLOTS)], 1)
        lanes = slice(half * BLK, (half + 1) * BLK)
        summed = jnp.dot(tiles, weights[:, lanes], preferred_element_type=jnp.float32)
        attended = (summed / total[:, lanes]).T.astype(jnp.bfloat16)
        cols = pl.ds(pl.multiple_of((head + half) * BLK, BLK), BLK)
        out_ref[side, :, cols] = attended


def pipelined(first, score, weigh, buffers):
    score_a, top_a, score_b, top_b = buffers
    last = first + CHUNK_COUPLES - 1
    score(first, score_a, top_a)

    def step(index, carry):
        couple = first + 2 * index
        score(couple + 1, score_b, top_b)
        weigh(couple, score_a, top_a)
        score(jnp.minimum(couple + 2, last), score_a, top_a)
        weigh(couple + 1, score_b, top_b)
        return carry

    lax.fori_loop(0, CHUNK_COUPLES // 2, step, 0)


BUFFERS = [pltpu.VMEM((SPAN, PAIR), jnp.float32), pltpu.VMEM((1, PAIR), jnp.float32)] * 2


def hold_kernel(source_ref, after_ref, out_ref, sem):
    copy = pltpu.make_async_copy(source_ref, out_ref, sem)
    copy.start()
    copy.wait()


def hold_call(source, after):
    return pl.pallas_call(
        hold_kernel,
        name="hold_weight",
        in_specs=[HBM, HBM],
        out_specs=VMEM,
        out_shape=pltpu.VMEM(source.shape, source.dtype),
        scratch_shapes=[pltpu.SemaphoreType.DMA],
        compiler_params=pltpu.CompilerParams(vmem_limit_bytes=4 * MIB),
    )(stay(source), after)


def prepare_kernel(place, key_ref, value_ref, mine_ref, theirs_ref):
    core = place[0]
    for out_ref, head in ((mine_ref, core), (theirs_ref, 1 - core)):
        for block in range(out_ref.shape[1]):
            rows = slice(block * BLK, (block + 1) * BLK)
            out_ref[0, block] = key_ref[head, rows, :]
            out_ref[1, block] = value_ref[head, rows, :].T


def prepare_call(place, keys, values):
    blocks = keys.shape[1] // BLK
    shape = jax.ShapeDtypeStruct((2, blocks, BLK, BLK), jnp.bfloat16)
    return pl.pallas_call(
        prepare_kernel,
        name="prepare",
        grid_spec=pltpu.PrefetchScalarGridSpec(
            num_scalar_prefetch=1, grid=(1,), in_specs=[VMEM] * 2, out_specs=[VMEM] * 2
        ),
        out_shape=[shape, shape],
        compiler_params=pltpu.CompilerParams(vmem_limit_bytes=6 * MIB),
    )(place, keys, values)


def bring(pieces, tables, sems, places):
    copies = []
    for index, (piece, (table, at)) in enumerate(zip(pieces, places)):
        copies.append(
            pltpu.make_async_copy(
                piece, tables[table].at[pl.ds(at, piece.shape[0])], sems.at[index]
            )
        )
    for copy in copies:
        copy.start()
    for copy in copies:
        copy.wait()


def tables_kernel(places, *refs):
    pieces, tables, sems = refs[: len(places)], refs[len(places) : -1], refs[-1]
    bring(pieces, tables, sems, places)


def tables_call(places, pieces):
    return pl.pallas_call(
        functools.partial(tables_kernel, places),
        name="tables",
        in_specs=[HBM] * len(pieces),
        out_specs=[VMEM] * 2,
        out_shape=[pltpu.VMEM((BLK, BLK, BLK), jnp.bfloat16)] * 2,
        scratch_shapes=[pltpu.SemaphoreType.DMA((len(pieces),))],
        compiler_params=pltpu.CompilerParams(vmem_limit_bytes=4 * MIB),
        cost_estimate=SHORT,
    )(*map(stay, pieces))


def attend_kernel(first, places, lists, counts, place, q_ref, after_ref, *refs):
    if places:
        pieces, refs = refs[: len(places)], refs[len(places) + 2 :]
        out_ref, keys, values, *buffers, sems = refs
        bring(pieces, (keys, values), sems, places)
    else:
        keys, values, out_ref, *buffers = refs

    def score(couple, score_ref, top_ref):
        score_couple(couple, lists, counts, place, q_ref, keys, score_ref, top_ref)

    def weigh(couple, score_ref, top_ref):
        tiles, total = weigh_couple(couple, counts, score_ref, top_ref)
        combine_couple(couple, cat(tiles, 0), total, lists, values, out_ref)

    pipelined(first, score, weigh, buffers)


def attend_call(name, chunk, lists, counts, place, queries, after, tables, pieces=(), places=()):
    out_shape = [jax.ShapeDtypeStruct((2, BLK, 8 * BLK), jnp.bfloat16)]
    scratch = list(BUFFERS)
    aliases = {}
    if pieces:
        out_shape += [pltpu.VMEM(table.shape, table.dtype) for table in tables]
        scratch += [pltpu.SemaphoreType.DMA((len(pieces),))]
        aliases = {5 + len(pieces): 1, 6 + len(pieces): 2}
    return pl.pallas_call(
        functools.partial(attend_kernel, chunk * CHUNK_COUPLES, places),
        name=name,
        grid_spec=pltpu.PrefetchScalarGridSpec(
            num_scalar_prefetch=3,
            grid=(1,),
            in_specs=[VMEM, VMEM if pieces else HBM] + [HBM] * len(pieces) + [VMEM] * len(tables),
            out_specs=[VMEM] * len(out_shape),
            scratch_shapes=scratch,
        ),
        out_shape=out_shape,
        input_output_aliases=aliases,
        compiler_params=pltpu.CompilerParams(vmem_limit_bytes=10 * MIB),
        cost_estimate=SHORT,
    )(lists, counts, place, queries, after, *map(stay, pieces), *tables)


def queries_kernel(place, source_ref, after_ref, mine_ref, theirs_ref, sems):
    heads = mine_ref.shape[0]
    core = place[0]
    copies = [
        pltpu.make_async_copy(
            source_ref.at[pl.ds(owner * heads, heads)], out_ref, sems.at[index]
        )
        for index, (owner, out_ref) in enumerate(((core, mine_ref), (1 - core, theirs_ref)))
    ]
    for copy in copies:
        copy.start()
    for copy in copies:
        copy.wait()


def queries_call(place, queries, heads, after):
    shape = jax.ShapeDtypeStruct((heads,) + queries.shape[1:], queries.dtype)
    return pl.pallas_call(
        queries_kernel,
        name="queries",
        grid_spec=pltpu.PrefetchScalarGridSpec(
            num_scalar_prefetch=1,
            grid=(1,),
            in_specs=[HBM, HBM],
            out_specs=[VMEM, VMEM],
            scratch_shapes=[pltpu.SemaphoreType.DMA((2,))],
        ),
        out_shape=[shape, shape],
        compiler_params=pltpu.CompilerParams(vmem_limit_bytes=8 * MIB),
        cost_estimate=SHORT,
    )(place, stay(queries), after)


def project_kernel(kind, place, mine_ref, theirs_ref, held_ref, after_ref, *refs):
    width = held_ref.shape[1]
    tile = 1024
    core = place[0]
    mine = mine_ref[...]
    theirs = theirs_ref[...]
    both = cat([jnp.where(core == 0, mine, theirs), jnp.where(core == 0, theirs, mine)], 1)
    for at in range(0, width, tile):
        cols = slice(at, at + tile)
        low = at < width // 2
        near = slice(at % (width // 2), at % (width // 2) + tile)
        total = jnp.dot(both, held_ref[:, cols], preferred_element_type=jnp.float32)
        if kind == "far":
            refs[0 if low else 1][:, near] = total.astype(jnp.bfloat16)
        elif kind == "own":
            refs[0][:, cols] = total
        else:
            if low == (kind == "up"):
                total = total + refs[0][:, near].astype(jnp.float32)
            refs[1][:, cols] = total.astype(jnp.bfloat16)


def project_call(kind, place, mine, theirs, held, after, *arrived):
    width = held.shape[1]
    shapes = {
        "far": [((BLK, width // 2), jnp.bfloat16)] * 2,
        "up": [((BLK, width), jnp.bfloat16)],
        "down": [((BLK, width), jnp.bfloat16)],
        "own": [((BLK, width), jnp.float32)],
    }[kind]
    return pl.pallas_call(
        functools.partial(project_kernel, kind),
        name="project_" + kind,
        grid_spec=pltpu.PrefetchScalarGridSpec(
            num_scalar_prefetch=1,
            grid=(1,),
            in_specs=[VMEM] * 3 + [HBM] + [VMEM] * len(arrived),
            out_specs=[VMEM] * len(shapes),
        ),
        out_shape=[jax.ShapeDtypeStruct(*shape) for shape in shapes],
        compiler_params=pltpu.CompilerParams(vmem_limit_bytes=8 * MIB),
        cost_estimate=SHORT,
    )(place, mine, theirs, held, after, *arrived)


def chip_perm(phase, step):
    pairs = []
    for z in range(RING):
        for y in range(RING):
            for core in range(CORES):
                if (core == 0) == (phase == 0):
                    to_z, to_y = z, (y + step) % RING
                else:
                    to_z, to_y = (z + step) % RING, y
                pairs.append(((z * RING + y) * CORES + core, (to_z * RING + to_y) * CORES + core))
    return pairs


SWAP = [(i, i ^ 1) for i in range(SEQ_DEVICES)]


def along(array, phase, step):
    return lax.ppermute(array, "seq", chip_perm(phase, step))


def swap(array):
    return lax.ppermute(array, "seq", SWAP)


def turn(array, step):
    return lax.ppermute(array, "grp", [(i, (i + step) % RING) for i in range(RING)])


def gather_tiles(own):
    parts = [own, along(own, 0, 1), along(own, 0, -1), along(own, 0, 2)]
    keys = cat([part[0] for part in parts], 0)
    values = cat([part[1] for part in parts], 0)
    keys_left, values_right = along(keys, 1, 1), along(values, 1, -1)
    values_left, keys_right = along(values, 1, 1), along(keys, 1, -1)
    keys_far, values_far = along(keys_left, 1, 1), along(values_right, 1, -1)
    size = keys.shape[0]
    early = [keys, keys_left, keys_right, values, values_left, values_right]
    early_places = ((0, 0), (0, size), (0, 2 * size), (1, 0), (1, size), (1, 2 * size))
    late = [keys_far, values_far]
    late_places = ((0, 3 * size), (1, 3 * size))
    return parts[1], early, early_places, late, late_places


def body(query_states, key_states, value_states, tile_keys, tile_count, out_weight):
    head_group, row_count, width = query_states.shape
    kv_group = key_states.shape[0]
    blocks = row_count // BLK
    heads = head_group // kv_group
    seq_place = lax.axis_index("seq")
    grp_place = lax.axis_index("grp")
    core = seq_place % CORES
    chip = seq_place // CORES
    chip_z, chip_y = chip // RING, chip % RING

    chunks = (grp_place + jnp.array([2, 1, 3, 0], jnp.int32)) % RING
    place = jnp.concatenate([core[None], chunks]).astype(jnp.int32)
    mine, theirs = prepare_call(place, key_states, value_states)
    first, early, early_places, late, late_places = gather_tiles(cat([mine, swap(theirs)], 1))

    queries_mine, queries_theirs = queries_call(place, query_states, heads, first)
    queries = jnp.stack([swap(queries_theirs), queries_mine])

    sides = jnp.stack([1 - core, core])
    order = (chip * 2 * blocks + sides[None, :] * blocks + chunks[:, None]).reshape(-1)
    my_lists = lax.dynamic_slice_in_dim(tile_keys, core * heads, heads, 0)
    my_counts = lax.dynamic_slice_in_dim(tile_count, core * heads, heads, 0)
    lists = jnp.swapaxes(jnp.take(my_lists, order, axis=1), 0, 1)
    counts = jnp.swapaxes(jnp.take(my_counts, order, axis=1), 0, 1).reshape(-1)

    span = 2 * blocks
    from_chip = lists // span
    inside = lists % span
    step_z = (from_chip // RING - chip_z) % RING
    step_y = (from_chip % RING - chip_y) % RING

    def arrival(step):
        return jnp.where(step == 1, 2, jnp.where(step == 2, 3, jnp.where(step == 3, 1, 0)))

    inner = arrival(jnp.where(core == 0, step_y, step_z))
    outer = arrival(jnp.where(core == 0, step_z, step_y))
    lists = (
        (outer * RING + inner) * span
        + (inside // blocks + core) % CORES * blocks
        + inside % blocks
    ).reshape(-1)

    held = hold_call(out_weight, first)

    tables = tables_call(early_places, early)
    far_att, *tables = attend_call(
        "attend_far", 0, lists, counts, place, queries, held, tables, late, late_places
    )

    def attend(name, chunk, after):
        return attend_call(name, chunk, lists, counts, place, queries, after, tables)

    low, high = project_call("far", place, far_att[1], swap(far_att[0]), held, far_att)
    low_in, high_in = turn(low, 1), turn(high, -1)
    (up_att,) = attend("attend_up", 1, low)
    (down_att,) = attend("attend_down", 2, up_att)
    (up,) = project_call("up", place, up_att[1], swap(up_att[0]), held, down_att, low_in)
    from_left = turn(up, 1)
    (down,) = project_call("down", place, down_att[1], swap(down_att[0]), held, up, high_in)
    from_right = turn(down, -1)
    (own_att,) = attend("attend_own", 3, down)
    (own,) = project_call("own", place, own_att[1], swap(own_att[0]), held, own_att)
    total = own + from_left.astype(jnp.float32) + from_right.astype(jnp.float32)
    return total.astype(jnp.bfloat16)


def solution(mesh):
    placed = (
        P("grp", "seq", None),
        P("grp", "seq", None),
        P("grp", "seq", None),
        P("grp", None, None),
        P("grp", None),
        P("grp", None),
    )
    return jax.shard_map(
        body, mesh=mesh, in_specs=placed, out_specs=P(("seq", "grp"), None), check_vma=False
    )
```

```python
import functools
import math

import jax
import jax.numpy as jnp
from jax import lax
from jax.experimental import pallas as pl
from jax.experimental.pallas import tpu as pltpu
from jax.sharding import PartitionSpec as P

BLK = 128
SLOTS = 16
PAIR = 2 * BLK
SPAN = SLOTS * BLK
RING = 4
CORES = 2
SEQ_DEVICES = RING * RING * CORES
SIDE_COUPLES = 4
CHUNK_COUPLES = 2 * SIDE_COUPLES
EXP2_SCALE = float(BLK ** -0.5 * math.log2(math.e))
LOW = -1e30
MIB = 2**20

SHORT = pl.CostEstimate(flops=1, bytes_accessed=1, transcendentals=0)
MIDDLE = pl.CostEstimate(flops=2 * 10**9, bytes_accessed=10**7, transcendentals=0)

VMEM = pl.BlockSpec(memory_space=pltpu.VMEM)
HBM = pl.BlockSpec(memory_space=pltpu.HBM)


def stay(array):
    return pltpu.with_memory_space_constraint(array, pltpu.HBM)


def cat(parts, axis):
    return jnp.concatenate(parts, axis)


def score_couple(couple, lists, counts, place, q_ref, table, score_ref, top_ref):
    key_row = lax.broadcasted_iota(jnp.int32, (BLK, PAIR), 0)
    query_row = lax.broadcasted_iota(jnp.int32, (BLK, PAIR), 1) % BLK
    zero = jnp.zeros((BLK, BLK), jnp.bfloat16)
    chunk = couple // CHUNK_COUPLES
    side = couple // SIDE_COUPLES % 2
    head = 2 * (couple % SIDE_COUPLES)
    rows = pl.ds(pl.multiple_of(place[1 + side * RING + chunk] * BLK, BLK), BLK)
    qa = q_ref[side, head, rows, :].T
    qb = q_ref[side, head + 1, rows, :].T
    queries = cat([cat([qa, zero], 1), cat([zero, qb], 1)], 0)
    a = 2 * couple * SLOTS
    keys = cat(
        [cat([table[lists[a + n]], table[lists[a + SLOTS + n]]], 1) for n in range(SLOTS)], 0
    )
    scores = jnp.dot(keys, queries, preferred_element_type=jnp.float32)
    count = live_counts(couple, counts)
    top = None
    for n in range(SLOTS):
        tile = scores[n * BLK : (n + 1) * BLK]
        if n == 0:
            tile = jnp.where(key_row <= query_row, tile, LOW)
            top = tile.reshape(16, 8, PAIR).max(0)
        else:
            best = tile.reshape(16, 8, PAIR).max(0)
            top = jnp.maximum(top, jnp.where(n < count, best, LOW))
        score_ref[n * BLK : (n + 1) * BLK, :] = tile
    top_ref[...] = jnp.max(top, axis=0, keepdims=True)


def live_counts(couple, counts):
    lane = lax.broadcasted_iota(jnp.int32, (1, PAIR), 1)
    return jnp.where(lane < BLK, counts[2 * couple], counts[2 * couple + 1])


def weigh_couple(couple, counts, score_ref, top_ref):
    count = live_counts(couple, counts)
    top = top_ref[...]
    total = jnp.zeros((8, PAIR), jnp.float32)
    tiles = []
    for n in range(SLOTS):
        shift = top if n == 0 else jnp.where(n < count, top, -LOW)
        weights = jnp.exp2((score_ref[n * BLK : (n + 1) * BLK, :] - shift) * EXP2_SCALE)
        total += weights.reshape(16, 8, PAIR).sum(0)
        tiles.append(weights.astype(jnp.bfloat16))
    return tiles, jnp.sum(total, axis=0, keepdims=True)


def combine_couple(couple, weights, total, lists, values, out_ref):
    head = 2 * (couple % SIDE_COUPLES)
    for half in range(2):
        pair = 2 * couple + half
        tiles = cat([values[lists[pair * SLOTS + n]] for n in range(SLOTS)], 1)
        lanes = slice(half * BLK, (half + 1) * BLK)
        summed = jnp.dot(tiles, weights[:, lanes], preferred_element_type=jnp.float32)
        attended = (summed / total[:, lanes]).T.astype(jnp.bfloat16)
        cols = pl.ds(pl.multiple_of((head + half) * BLK, BLK), BLK)
        out_ref[:, cols] = attended


def pipelined(first, score, weigh, buffers):
    score_a, top_a, score_b, top_b = buffers
    score(first, score_a, top_a)

    def step(index, carry):
        couple = first + 2 * index
        score(couple + 1, score_b, top_b)
        weigh(couple, score_a, top_a)
        score(couple + 2, score_a, top_a)
        weigh(couple + 1, score_b, top_b)
        return carry

    lax.fori_loop(0, SIDE_COUPLES // 2 - 1, step, 0)
    last = first + SIDE_COUPLES - 1
    score(last, score_b, top_b)
    weigh(last - 1, score_a, top_a)
    weigh(last, score_b, top_b)


BUFFERS = [pltpu.VMEM((SPAN, PAIR), jnp.float32), pltpu.VMEM((1, PAIR), jnp.float32)] * 2


def hold_kernel(source_ref, after_ref, out_ref, sem):
    copy = pltpu.make_async_copy(source_ref, out_ref, sem)
    copy.start()
    copy.wait()


def hold_call(source, after):
    return pl.pallas_call(
        hold_kernel,
        name="hold_weight",
        in_specs=[HBM, HBM],
        out_specs=VMEM,
        out_shape=pltpu.VMEM(source.shape, source.dtype),
        scratch_shapes=[pltpu.SemaphoreType.DMA],
        compiler_params=pltpu.CompilerParams(vmem_limit_bytes=4 * MIB),
    )(stay(source), after)


def prepare_kernel(place, key_ref, value_ref, mine_ref, theirs_ref):
    core = place[0]
    for out_ref, head in ((mine_ref, core), (theirs_ref, 1 - core)):
        for block in range(out_ref.shape[1]):
            rows = slice(block * BLK, (block + 1) * BLK)
            out_ref[0, block] = key_ref[head, rows, :]
            out_ref[1, block] = value_ref[head, rows, :].T


def prepare_call(place, keys, values):
    blocks = keys.shape[1] // BLK
    shape = jax.ShapeDtypeStruct((2, blocks, BLK, BLK), jnp.bfloat16)
    return pl.pallas_call(
        prepare_kernel,
        name="prepare",
        grid_spec=pltpu.PrefetchScalarGridSpec(
            num_scalar_prefetch=1, grid=(1,), in_specs=[VMEM] * 2, out_specs=[VMEM] * 2
        ),
        out_shape=[shape, shape],
        compiler_params=pltpu.CompilerParams(vmem_limit_bytes=6 * MIB),
    )(place, keys, values)


def bring(pieces, tables, sems, places):
    copies = []
    for index, (piece, (table, at)) in enumerate(zip(pieces, places)):
        copies.append(
            pltpu.make_async_copy(
                piece, tables[table].at[pl.ds(at, piece.shape[0])], sems.at[index]
            )
        )
    for copy in copies:
        copy.start()
    for copy in copies:
        copy.wait()


def tables_kernel(places, *refs):
    pieces, tables, sems = refs[: len(places)], refs[len(places) : -1], refs[-1]
    bring(pieces, tables, sems, places)


def tables_call(places, pieces):
    return pl.pallas_call(
        functools.partial(tables_kernel, places),
        name="tables",
        in_specs=[HBM] * len(pieces),
        out_specs=[VMEM] * 2,
        out_shape=[pltpu.VMEM((BLK, BLK, BLK), jnp.bfloat16)] * 2,
        scratch_shapes=[pltpu.SemaphoreType.DMA((len(pieces),))],
        compiler_params=pltpu.CompilerParams(vmem_limit_bytes=4 * MIB),
        cost_estimate=SHORT,
    )(*map(stay, pieces))


def attend_kernel(first, places, lists, counts, place, q_ref, after_ref, also_ref, *refs):
    if places:
        pieces, refs = refs[: len(places)], refs[len(places) + 2 :]
        out_ref, keys, values, *buffers, sems = refs
        bring(pieces, (keys, values), sems, places)
    else:
        keys, values, out_ref, *buffers = refs

    def score(couple, score_ref, top_ref):
        score_couple(couple, lists, counts, place, q_ref, keys, score_ref, top_ref)

    def weigh(couple, score_ref, top_ref):
        tiles, total = weigh_couple(couple, counts, score_ref, top_ref)
        combine_couple(couple, cat(tiles, 0), total, lists, values, out_ref)

    pipelined(first, score, weigh, buffers)


def attend_call(
    name, chunk, side, lists, counts, place, queries, after, tables, pieces=(), places=(), cost=SHORT
):
    out_shape = [jax.ShapeDtypeStruct((BLK, 8 * BLK), jnp.bfloat16)]
    scratch = list(BUFFERS)
    aliases = {}
    if pieces:
        out_shape += [pltpu.VMEM(table.shape, table.dtype) for table in tables]
        scratch += [pltpu.SemaphoreType.DMA((len(pieces),))]
        aliases = {6 + len(pieces): 1, 7 + len(pieces): 2}
    return pl.pallas_call(
        functools.partial(attend_kernel, chunk * CHUNK_COUPLES + side * SIDE_COUPLES, places),
        name=name,
        grid_spec=pltpu.PrefetchScalarGridSpec(
            num_scalar_prefetch=3,
            grid=(1,),
            in_specs=[VMEM] + [VMEM if pieces else HBM] * 2 + [HBM] * len(pieces) + [VMEM] * len(tables),
            out_specs=[VMEM] * len(out_shape),
            scratch_shapes=scratch,
        ),
        out_shape=out_shape,
        input_output_aliases=aliases,
        compiler_params=pltpu.CompilerParams(vmem_limit_bytes=10 * MIB),
        cost_estimate=cost,
    )(lists, counts, place, queries, *after, *map(stay, pieces), *tables)


def queries_kernel(place, source_ref, after_ref, mine_ref, theirs_ref, sems):
    heads = mine_ref.shape[0]
    core = place[0]
    copies = [
        pltpu.make_async_copy(
            source_ref.at[pl.ds(owner * heads, heads)], out_ref, sems.at[index]
        )
        for index, (owner, out_ref) in enumerate(((core, mine_ref), (1 - core, theirs_ref)))
    ]
    for copy in copies:
        copy.start()
    for copy in copies:
        copy.wait()


def queries_call(place, queries, heads, after):
    shape = jax.ShapeDtypeStruct((heads,) + queries.shape[1:], queries.dtype)
    return pl.pallas_call(
        queries_kernel,
        name="queries",
        grid_spec=pltpu.PrefetchScalarGridSpec(
            num_scalar_prefetch=1,
            grid=(1,),
            in_specs=[HBM, HBM],
            out_specs=[VMEM, VMEM],
            scratch_shapes=[pltpu.SemaphoreType.DMA((2,))],
        ),
        out_shape=[shape, shape],
        compiler_params=pltpu.CompilerParams(vmem_limit_bytes=8 * MIB),
        cost_estimate=SHORT,
    )(place, stay(queries), after)


def project_kernel(kind, place, mine_ref, theirs_ref, held_ref, after_ref, *refs):
    out_ref = refs[-1]
    width = held_ref.shape[1]
    tile = 1024
    core = place[0]
    mine = mine_ref[...]
    theirs = theirs_ref[...]
    both = cat([jnp.where(core == 0, mine, theirs), jnp.where(core == 0, theirs, mine)], 1)
    for at in range(0, width, tile):
        cols = slice(at, at + tile)
        total = jnp.dot(both, held_ref[:, cols], preferred_element_type=jnp.float32)
        if kind in ("first", "own"):
            total = total + refs[0][:, cols].astype(jnp.float32)
        out_ref[:, cols] = total.astype(out_ref.dtype)


def project_call(kind, place, mine, theirs, held, after, *arrived):
    width = held.shape[1]
    out_type = jnp.float32 if kind == "own" else jnp.bfloat16
    return pl.pallas_call(
        functools.partial(project_kernel, kind),
        name="project_" + kind,
        grid_spec=pltpu.PrefetchScalarGridSpec(
            num_scalar_prefetch=1,
            grid=(1,),
            in_specs=[VMEM] * 3 + [HBM] + [VMEM] * len(arrived),
            out_specs=VMEM,
        ),
        out_shape=jax.ShapeDtypeStruct((BLK, width), out_type),
        compiler_params=pltpu.CompilerParams(vmem_limit_bytes=8 * MIB),
        cost_estimate=MIDDLE if kind == "own" else SHORT,
    )(place, mine, theirs, held, after, *arrived)


def chip_perm(phase, step):
    pairs = []
    for z in range(RING):
        for y in range(RING):
            for core in range(CORES):
                if (core == 0) == (phase == 0):
                    to_z, to_y = z, (y + step) % RING
                else:
                    to_z, to_y = (z + step) % RING, y
                pairs.append(((z * RING + y) * CORES + core, (to_z * RING + to_y) * CORES + core))
    return pairs


SWAP = [(i, i ^ 1) for i in range(SEQ_DEVICES)]


def along(array, phase, step):
    return lax.ppermute(array, "seq", chip_perm(phase, step))


def swap(array):
    return lax.ppermute(array, "seq", SWAP)


def turn(array, step):
    pairs = []
    for seq in range(SEQ_DEVICES):
        way = step if seq % CORES == 0 else -step
        pairs += [(seq * RING + i, seq * RING + (i + way) % RING) for i in range(RING)]
    return lax.ppermute(array, ("seq", "grp"), pairs)


def gather_tiles(own):
    parts = [own, along(own, 0, 1), along(own, 0, -1), along(own, 0, 2)]
    keys = cat([part[0] for part in parts], 0)
    values = cat([part[1] for part in parts], 0)
    keys_left, values_right = along(keys, 1, 1), along(values, 1, -1)
    values_left, keys_right = along(values, 1, 1), along(keys, 1, -1)
    keys_far, values_far = along(keys_left, 1, 1), along(values_right, 1, -1)
    size = keys.shape[0]
    early = [keys, keys_left, keys_right, values, values_left, values_right]
    early_places = ((0, 0), (0, size), (0, 2 * size), (1, 0), (1, size), (1, 2 * size))
    late = [keys_far, values_far]
    late_places = ((0, 3 * size), (1, 3 * size))
    return parts[1], early, early_places, late, late_places


def body(query_states, key_states, value_states, tile_keys, tile_count, out_weight):
    head_group, row_count, width = query_states.shape
    kv_group = key_states.shape[0]
    blocks = row_count // BLK
    heads = head_group // kv_group
    seq_place = lax.axis_index("seq")
    grp_place = lax.axis_index("grp")
    core = seq_place % CORES
    chip = seq_place // CORES
    chip_z, chip_y = chip // RING, chip % RING

    ways = jnp.array([[2, 1, 3, 0], [2, 3, 1, 0]], jnp.int32)
    mine_chunks = jnp.where(core == 0, ways[0], ways[1])
    theirs_chunks = jnp.where(core == 0, ways[1], ways[0])
    chunks = (grp_place + jnp.stack([theirs_chunks, mine_chunks])) % RING
    place = jnp.concatenate([core[None], chunks.reshape(-1)]).astype(jnp.int32)
    mine, theirs = prepare_call(place, key_states, value_states)
    neighbor, early, early_places, late, late_places = gather_tiles(cat([mine, swap(theirs)], 1))

    queries_mine, queries_theirs = queries_call(place, query_states, heads, neighbor)
    queries = jnp.stack([swap(queries_theirs), queries_mine])

    sides = jnp.stack([1 - core, core])
    order = (chip * 2 * blocks + sides[None, :] * blocks + chunks.T).reshape(-1)
    my_lists = lax.dynamic_slice_in_dim(tile_keys, core * heads, heads, 0)
    my_counts = lax.dynamic_slice_in_dim(tile_count, core * heads, heads, 0)
    lists = jnp.swapaxes(jnp.take(my_lists, order, axis=1), 0, 1)
    counts = jnp.swapaxes(jnp.take(my_counts, order, axis=1), 0, 1).reshape(-1)

    span = 2 * blocks
    from_chip = lists // span
    inside = lists % span
    step_z = (from_chip // RING - chip_z) % RING
    step_y = (from_chip % RING - chip_y) % RING

    def arrival(step):
        return jnp.where(step == 1, 2, jnp.where(step == 2, 3, jnp.where(step == 3, 1, 0)))

    inner = arrival(jnp.where(core == 0, step_y, step_z))
    outer = arrival(jnp.where(core == 0, step_z, step_y))
    lists = (
        (outer * RING + inner) * span
        + (inside // blocks + core) % CORES * blocks
        + inside % blocks
    ).reshape(-1)

    held = hold_call(out_weight, neighbor)

    tables = tables_call(early_places, early)
    far_theirs, *tables = attend_call(
        "far_theirs", 0, 0, lists, counts, place, queries, (held, held), tables, late, late_places
    )

    def attend(name, chunk, side, after, cost=SHORT):
        (out,) = attend_call(
            name, chunk, side, lists, counts, place, queries, after, tables, cost=cost
        )
        return out

    far_mine = attend("far_mine", 0, 1, (far_theirs, far_theirs))
    far = project_call("far", place, far_mine, swap(far_theirs), held, far_mine)
    passed = turn(far, 1)
    first_theirs = attend("first_theirs", 1, 0, (far, far))
    first_mine = attend("first_mine", 1, 1, (first_theirs, first_theirs))
    second_theirs = attend("second_theirs", 2, 0, (first_mine, first_mine))
    first = project_call(
        "first", place, first_mine, swap(first_theirs), held, second_theirs, passed
    )
    arrived = turn(first, 1)
    second_mine = attend("second_mine", 2, 1, (first, first))
    second = project_call(
        "second", place, second_mine, swap(second_theirs), held, second_mine
    )
    arrived_last = turn(second, -1)
    own_theirs = attend("own_theirs", 3, 0, (second, second))
    own_mine = attend("own_mine", 3, 1, (own_theirs, own_theirs))
    own = project_call("own", place, own_mine, swap(own_theirs), held, own_mine, arrived)
    total = own + arrived_last.astype(jnp.float32)
    return total.astype(jnp.bfloat16)


def solution(mesh):
    placed = (
        P("grp", "seq", None),
        P("grp", "seq", None),
        P("grp", "seq", None),
        P("grp", None, None),
        P("grp", None),
        P("grp", None),
    )
    return jax.shard_map(
        body, mesh=mesh, in_specs=placed, out_specs=P(("seq", "grp"), None), check_vma=False
    )
```

```python
import functools
import math

import jax
import jax.numpy as jnp
from jax import lax
from jax.experimental import pallas as pl
from jax.experimental.pallas import tpu as pltpu
from jax.sharding import PartitionSpec as P

BLK = 128
SLOTS = 16
PAIR = 2 * BLK
SPAN = SLOTS * BLK
RING = 4
CORES = 2
SEQ_DEVICES = RING * RING * CORES
SIDE_COUPLES = 4
CHUNK_COUPLES = 2 * SIDE_COUPLES
EXP2_SCALE = float(BLK ** -0.5 * math.log2(math.e))
LOW = -1e30
MIB = 2**20

SHORT = pl.CostEstimate(flops=1, bytes_accessed=1, transcendentals=0)
MIDDLE = pl.CostEstimate(flops=2 * 10**9, bytes_accessed=10**7, transcendentals=0)

VMEM = pl.BlockSpec(memory_space=pltpu.VMEM)
HBM = pl.BlockSpec(memory_space=pltpu.HBM)


def stay(array):
    return pltpu.with_memory_space_constraint(array, pltpu.HBM)


def cat(parts, axis):
    return jnp.concatenate(parts, axis)


def score_couple(couple, lists, counts, place, q_ref, table, score_ref, top_ref):
    key_row = lax.broadcasted_iota(jnp.int32, (BLK, PAIR), 0)
    query_row = lax.broadcasted_iota(jnp.int32, (BLK, PAIR), 1) % BLK
    zero = jnp.zeros((BLK, BLK), jnp.bfloat16)
    chunk = couple // CHUNK_COUPLES
    side = couple // SIDE_COUPLES % 2
    head = 2 * (couple % SIDE_COUPLES)
    rows = pl.ds(pl.multiple_of(place[1 + side * RING + chunk] * BLK, BLK), BLK)
    qa = q_ref[side, head, rows, :].T
    qb = q_ref[side, head + 1, rows, :].T
    queries = cat([cat([qa, zero], 1), cat([zero, qb], 1)], 0)
    a = 2 * couple * SLOTS
    keys = cat(
        [cat([table[lists[a + n]], table[lists[a + SLOTS + n]]], 1) for n in range(SLOTS)], 0
    )
    scores = jnp.dot(keys, queries, preferred_element_type=jnp.float32)
    count = live_counts(couple, counts)
    top = None
    for n in range(SLOTS):
        tile = scores[n * BLK : (n + 1) * BLK]
        if n == 0:
            tile = jnp.where(key_row <= query_row, tile, LOW)
            top = tile.reshape(16, 8, PAIR).max(0)
        else:
            best = tile.reshape(16, 8, PAIR).max(0)
            top = jnp.maximum(top, jnp.where(n < count, best, LOW))
        score_ref[n * BLK : (n + 1) * BLK, :] = tile
    top_ref[...] = jnp.max(top, axis=0, keepdims=True)


def live_counts(couple, counts):
    lane = lax.broadcasted_iota(jnp.int32, (1, PAIR), 1)
    return jnp.where(lane < BLK, counts[2 * couple], counts[2 * couple + 1])


def weigh_couple(couple, counts, score_ref, top_ref):
    count = live_counts(couple, counts)
    top = top_ref[...]
    total = jnp.zeros((8, PAIR), jnp.float32)
    tiles = []
    for n in range(SLOTS):
        shift = top if n == 0 else jnp.where(n < count, top, -LOW)
        weights = jnp.exp2((score_ref[n * BLK : (n + 1) * BLK, :] - shift) * EXP2_SCALE)
        total += weights.reshape(16, 8, PAIR).sum(0)
        tiles.append(weights.astype(jnp.bfloat16))
    return tiles, jnp.sum(total, axis=0, keepdims=True)


def combine_couple(couple, weights, total, lists, values, out_ref):
    head = 2 * (couple % SIDE_COUPLES)
    for half in range(2):
        pair = 2 * couple + half
        tiles = cat([values[lists[pair * SLOTS + n]] for n in range(SLOTS)], 1)
        lanes = slice(half * BLK, (half + 1) * BLK)
        summed = jnp.dot(tiles, weights[:, lanes], preferred_element_type=jnp.float32)
        attended = (summed / total[:, lanes]).T.astype(jnp.bfloat16)
        cols = pl.ds(pl.multiple_of((head + half) * BLK, BLK), BLK)
        out_ref[:, cols] = attended


def pipelined(first, score, weigh, buffers, rest):
    score_a, top_a, score_b, top_b = buffers
    score(first, score_a, top_a)
    for copy in rest:
        copy.wait()

    last = first + SIDE_COUPLES - 1

    def step(index, carry):
        couple = first + 2 * index
        score(couple + 1, score_b, top_b)
        weigh(couple, score_a, top_a)
        score(jnp.minimum(couple + 2, last), score_a, top_a)
        weigh(couple + 1, score_b, top_b)
        return carry

    lax.fori_loop(0, SIDE_COUPLES // 2, step, 0)


BUFFERS = [pltpu.VMEM((SPAN, PAIR), jnp.float32), pltpu.VMEM((1, PAIR), jnp.float32)] * 2


def hold_kernel(source_ref, after_ref, out_ref, sem):
    copy = pltpu.make_async_copy(source_ref, out_ref, sem)
    copy.start()
    copy.wait()


def hold_call(source, after):
    return pl.pallas_call(
        hold_kernel,
        name="hold_weight",
        in_specs=[HBM, HBM],
        out_specs=VMEM,
        out_shape=pltpu.VMEM(source.shape, source.dtype),
        scratch_shapes=[pltpu.SemaphoreType.DMA],
        compiler_params=pltpu.CompilerParams(vmem_limit_bytes=4 * MIB),
    )(stay(source), after)


def prepare_kernel(key_ref, value_ref, mine_ref, theirs_ref, key_held, value_held, sems):
    core = lax.rem(lax.axis_index("seq"), CORES)
    copies = [
        pltpu.make_async_copy(key_ref, key_held, sems.at[0]),
        pltpu.make_async_copy(value_ref, value_held, sems.at[1]),
    ]
    for copy in copies:
        copy.start()
    for copy in copies:
        copy.wait()
    for out_ref, head in ((mine_ref, core), (theirs_ref, 1 - core)):
        for block in range(out_ref.shape[1]):
            rows = slice(block * BLK, (block + 1) * BLK)
            out_ref[0, block] = key_held[head, rows, :]
            out_ref[1, block] = value_held[head, rows, :].T


def prepare_call(keys, values):
    blocks = keys.shape[1] // BLK
    shape = jax.ShapeDtypeStruct((2, blocks, BLK, BLK), jnp.bfloat16)
    return pl.pallas_call(
        prepare_kernel,
        name="prepare",
        in_specs=[HBM] * 2,
        out_specs=[VMEM] * 2,
        out_shape=[shape, shape],
        scratch_shapes=[pltpu.VMEM(keys.shape, keys.dtype)] * 2
        + [pltpu.SemaphoreType.DMA((2,))],
        compiler_params=pltpu.CompilerParams(vmem_limit_bytes=6 * MIB),
        cost_estimate=SHORT,
    )(stay(keys), stay(values))


def bring(pieces, tables, sems, places):
    copies = []
    for index, (piece, (table, at)) in enumerate(zip(pieces, places)):
        copies.append(
            pltpu.make_async_copy(
                piece, tables[table].at[pl.ds(at, piece.shape[0])], sems.at[index]
            )
        )
    for copy in copies:
        copy.start()
    return copies


def tables_kernel(places, *refs):
    pieces, tables, sems = refs[: len(places)], refs[len(places) : -1], refs[-1]
    for copy in bring(pieces, tables, sems, places):
        copy.wait()


def tables_call(places, pieces):
    return pl.pallas_call(
        functools.partial(tables_kernel, places),
        name="tables",
        in_specs=[HBM] * len(pieces),
        out_specs=[VMEM] * 2,
        out_shape=[pltpu.VMEM((BLK, BLK, BLK), jnp.bfloat16)] * 2,
        scratch_shapes=[pltpu.SemaphoreType.DMA((len(pieces),))],
        compiler_params=pltpu.CompilerParams(vmem_limit_bytes=4 * MIB),
        cost_estimate=SHORT,
    )(*map(stay, pieces))


def attend_kernel(first, places, lists, counts, place, q_ref, after_ref, also_ref, *refs):
    if places:
        pieces, refs = refs[: len(places)], refs[len(places) + 2 :]
        out_ref, keys, values, *buffers, sems = refs
        copies = bring(pieces, (keys, values), sems, places)
        copies[0].wait()
        rest = copies[1:]
    else:
        keys, values, out_ref, *buffers = refs
        rest = []

    def score(couple, score_ref, top_ref):
        score_couple(couple, lists, counts, place, q_ref, keys, score_ref, top_ref)

    def weigh(couple, score_ref, top_ref):
        tiles, total = weigh_couple(couple, counts, score_ref, top_ref)
        combine_couple(couple, cat(tiles, 0), total, lists, values, out_ref)

    pipelined(first, score, weigh, buffers, rest)


def attend_call(
    name, chunk, side, lists, counts, place, queries, after, tables, pieces=(), places=(), cost=SHORT
):
    out_shape = [jax.ShapeDtypeStruct((BLK, 8 * BLK), jnp.bfloat16)]
    scratch = list(BUFFERS)
    aliases = {}
    if pieces:
        out_shape += [pltpu.VMEM(table.shape, table.dtype) for table in tables]
        scratch += [pltpu.SemaphoreType.DMA((len(pieces),))]
        aliases = {6 + len(pieces): 1, 7 + len(pieces): 2}
    return pl.pallas_call(
        functools.partial(attend_kernel, chunk * CHUNK_COUPLES + side * SIDE_COUPLES, places),
        name=name,
        grid_spec=pltpu.PrefetchScalarGridSpec(
            num_scalar_prefetch=3,
            grid=(1,),
            in_specs=[VMEM] + [VMEM if pieces else HBM] * 2 + [HBM] * len(pieces) + [VMEM] * len(tables),
            out_specs=[VMEM] * len(out_shape),
            scratch_shapes=scratch,
        ),
        out_shape=out_shape,
        input_output_aliases=aliases,
        compiler_params=pltpu.CompilerParams(vmem_limit_bytes=10 * MIB),
        cost_estimate=cost,
    )(lists, counts, place, queries, *after, *map(stay, pieces), *tables)


def queries_kernel(place, source_ref, after_ref, mine_ref, theirs_ref, sems):
    heads = mine_ref.shape[0]
    core = place[0]
    copies = [
        pltpu.make_async_copy(
            source_ref.at[pl.ds(owner * heads, heads)], out_ref, sems.at[index]
        )
        for index, (owner, out_ref) in enumerate(((core, mine_ref), (1 - core, theirs_ref)))
    ]
    for copy in copies:
        copy.start()
    for copy in copies:
        copy.wait()


def queries_call(place, queries, heads, after):
    shape = jax.ShapeDtypeStruct((heads,) + queries.shape[1:], queries.dtype)
    return pl.pallas_call(
        queries_kernel,
        name="queries",
        grid_spec=pltpu.PrefetchScalarGridSpec(
            num_scalar_prefetch=1,
            grid=(1,),
            in_specs=[HBM, HBM],
            out_specs=[VMEM, VMEM],
            scratch_shapes=[pltpu.SemaphoreType.DMA((2,))],
        ),
        out_shape=[shape, shape],
        compiler_params=pltpu.CompilerParams(vmem_limit_bytes=8 * MIB),
        cost_estimate=SHORT,
    )(place, stay(queries), after)


def project_kernel(kind, place, mine_ref, theirs_ref, held_ref, after_ref, *refs):
    out_ref = refs[-1]
    width = held_ref.shape[1]
    tile = 1024
    core = place[0]
    mine = mine_ref[...]
    theirs = theirs_ref[...]
    both = cat([jnp.where(core == 0, mine, theirs), jnp.where(core == 0, theirs, mine)], 1)
    for at in range(0, width, tile):
        cols = slice(at, at + tile)
        total = jnp.dot(both, held_ref[:, cols], preferred_element_type=jnp.float32)
        if kind in ("first", "own"):
            total = total + refs[0][:, cols].astype(jnp.float32)
        out_ref[:, cols] = total.astype(out_ref.dtype)


def project_call(kind, place, mine, theirs, held, after, *arrived):
    width = held.shape[1]
    out_type = jnp.float32 if kind == "own" else jnp.bfloat16
    return pl.pallas_call(
        functools.partial(project_kernel, kind),
        name="project_" + kind,
        grid_spec=pltpu.PrefetchScalarGridSpec(
            num_scalar_prefetch=1,
            grid=(1,),
            in_specs=[VMEM] * 3 + [HBM] + [VMEM] * len(arrived),
            out_specs=VMEM,
        ),
        out_shape=jax.ShapeDtypeStruct((BLK, width), out_type),
        compiler_params=pltpu.CompilerParams(vmem_limit_bytes=8 * MIB),
        cost_estimate=MIDDLE if kind == "own" else SHORT,
    )(place, mine, theirs, held, after, *arrived)


def chip_perm(phase, step):
    pairs = []
    for z in range(RING):
        for y in range(RING):
            for core in range(CORES):
                if (core == 0) == (phase == 0):
                    to_z, to_y = z, (y + step) % RING
                else:
                    to_z, to_y = (z + step) % RING, y
                pairs.append(((z * RING + y) * CORES + core, (to_z * RING + to_y) * CORES + core))
    return pairs


SWAP = [(i, i ^ 1) for i in range(SEQ_DEVICES)]


def along(array, phase, step):
    return lax.ppermute(array, "seq", chip_perm(phase, step))


def swap(array):
    return lax.ppermute(array, "seq", SWAP)


def turn(array, step):
    pairs = []
    for seq in range(SEQ_DEVICES):
        way = step if seq % CORES == 0 else -step
        pairs += [(seq * RING + i, seq * RING + (i + way) % RING) for i in range(RING)]
    return lax.ppermute(array, ("seq", "grp"), pairs)


def gather_tiles(own):
    parts = [own, along(own, 0, 1), along(own, 0, -1), along(own, 0, 2)]
    keys = cat([part[0] for part in parts], 0)
    values = cat([part[1] for part in parts], 0)
    keys_left, values_right = along(keys, 1, 1), along(values, 1, -1)
    values_left, keys_right = along(values, 1, 1), along(keys, 1, -1)
    keys_far, values_far = along(keys_left, 1, 1), along(values_right, 1, -1)
    size = keys.shape[0]
    early = [keys, keys_left, keys_right, values, values_left, values_right]
    early_places = ((0, 0), (0, size), (0, 2 * size), (1, 0), (1, size), (1, 2 * size))
    late = [keys_far, values_far]
    late_places = ((0, 3 * size), (1, 3 * size))
    return parts[1], early, early_places, late, late_places


def body(query_states, key_states, value_states, tile_keys, tile_count, out_weight):
    head_group, row_count, width = query_states.shape
    kv_group = key_states.shape[0]
    blocks = row_count // BLK
    heads = head_group // kv_group
    seq_place = lax.axis_index("seq")
    grp_place = lax.axis_index("grp")
    core = seq_place % CORES
    chip = seq_place // CORES
    chip_z, chip_y = chip // RING, chip % RING

    ways = jnp.array([[2, 1, 3, 0], [2, 3, 1, 0]], jnp.int32)
    mine_chunks = jnp.where(core == 0, ways[0], ways[1])
    theirs_chunks = jnp.where(core == 0, ways[1], ways[0])
    chunks = (grp_place + jnp.stack([theirs_chunks, mine_chunks])) % RING
    place = jnp.concatenate([core[None], chunks.reshape(-1)]).astype(jnp.int32)
    mine, theirs = prepare_call(key_states, value_states)
    neighbor, early, early_places, late, late_places = gather_tiles(cat([mine, swap(theirs)], 1))

    queries_mine, queries_theirs = queries_call(place, query_states, heads, neighbor)
    queries = jnp.stack([swap(queries_theirs), queries_mine])

    sides = jnp.stack([1 - core, core])
    order = (chip * 2 * blocks + sides[None, :] * blocks + chunks.T).reshape(-1)
    my_lists = lax.dynamic_slice_in_dim(tile_keys, core * heads, heads, 0)
    my_counts = lax.dynamic_slice_in_dim(tile_count, core * heads, heads, 0)
    lists = jnp.swapaxes(jnp.take(my_lists, order, axis=1), 0, 1)
    counts = jnp.swapaxes(jnp.take(my_counts, order, axis=1), 0, 1).reshape(-1)

    span = 2 * blocks
    from_chip = lists // span
    inside = lists % span
    step_z = (from_chip // RING - chip_z) % RING
    step_y = (from_chip % RING - chip_y) % RING

    def arrival(step):
        return jnp.where(step == 1, 2, jnp.where(step == 2, 3, jnp.where(step == 3, 1, 0)))

    inner = arrival(jnp.where(core == 0, step_y, step_z))
    outer = arrival(jnp.where(core == 0, step_z, step_y))
    lists = (
        (outer * RING + inner) * span
        + (inside // blocks + core) % CORES * blocks
        + inside % blocks
    ).reshape(-1)

    held = hold_call(out_weight, neighbor)

    tables = tables_call(early_places, early)
    far_theirs, *tables = attend_call(
        "far_theirs", 0, 0, lists, counts, place, queries, (held, held), tables, late, late_places
    )

    def attend(name, chunk, side, after, cost=SHORT):
        (out,) = attend_call(
            name, chunk, side, lists, counts, place, queries, after, tables, cost=cost
        )
        return out

    far_mine = attend("far_mine", 0, 1, (far_theirs, far_theirs))
    far = project_call("far", place, far_mine, swap(far_theirs), held, far_mine)
    passed = turn(far, 1)
    first_theirs = attend("first_theirs", 1, 0, (far, far))
    first_mine = attend("first_mine", 1, 1, (first_theirs, first_theirs))
    second_theirs = attend("second_theirs", 2, 0, (first_mine, first_mine))
    first = project_call(
        "first", place, first_mine, swap(first_theirs), held, second_theirs, passed
    )
    arrived = turn(first, 1)
    second_mine = attend("second_mine", 2, 1, (first, first))
    second = project_call(
        "second", place, second_mine, swap(second_theirs), held, second_mine
    )
    arrived_last = turn(second, -1)
    own_theirs = attend("own_theirs", 3, 0, (second, second))
    own_mine = attend("own_mine", 3, 1, (own_theirs, own_theirs))
    own = project_call("own", place, own_mine, swap(own_theirs), held, own_mine, arrived)
    total = own + arrived_last.astype(jnp.float32)
    return total.astype(jnp.bfloat16)


def solution(mesh):
    placed = (
        P("grp", "seq", None),
        P("grp", "seq", None),
        P("grp", "seq", None),
        P("grp", None, None),
        P("grp", None),
        P("grp", None),
    )
    return jax.shard_map(
        body, mesh=mesh, in_specs=placed, out_specs=P(("seq", "grp"), None), check_vma=False
    )
```

```python
import functools
import math

import jax
import jax.numpy as jnp
from jax import lax
from jax.experimental import pallas as pl
from jax.experimental.pallas import tpu as pltpu
from jax.sharding import PartitionSpec as P

BLK = 128
SLOTS = 16
PAIR = 2 * BLK
SPAN = SLOTS * BLK
RING = 4
CORES = 2
SEQ_DEVICES = RING * RING * CORES
SIDE_COUPLES = 4
CHUNK_COUPLES = 2 * SIDE_COUPLES
EXP2_SCALE = float(BLK ** -0.5 * math.log2(math.e))
LOW = -1e30
MIB = 2**20

SHORT = pl.CostEstimate(flops=1, bytes_accessed=1, transcendentals=0)
MIDDLE = pl.CostEstimate(flops=2 * 10**9, bytes_accessed=10**7, transcendentals=0)

VMEM = pl.BlockSpec(memory_space=pltpu.VMEM)
HBM = pl.BlockSpec(memory_space=pltpu.HBM)


def stay(array):
    return pltpu.with_memory_space_constraint(array, pltpu.HBM)


def cat(parts, axis):
    return jnp.concatenate(parts, axis)


def score_couple(couple, lists, counts, place, q_ref, table, score_ref, top_ref):
    key_row = lax.broadcasted_iota(jnp.int32, (BLK, PAIR), 0)
    query_row = lax.broadcasted_iota(jnp.int32, (BLK, PAIR), 1) % BLK
    zero = jnp.zeros((BLK, BLK), jnp.bfloat16)
    chunk = couple // CHUNK_COUPLES
    side = couple // SIDE_COUPLES % 2
    head = 2 * (couple % SIDE_COUPLES)
    rows = pl.ds(pl.multiple_of(place[1 + side * RING + chunk] * BLK, BLK), BLK)
    qa = q_ref[side, head, rows, :].T
    qb = q_ref[side, head + 1, rows, :].T
    queries = cat([cat([qa, zero], 1), cat([zero, qb], 1)], 0)
    a = 2 * couple * SLOTS
    keys = cat(
        [cat([table[lists[a + n]], table[lists[a + SLOTS + n]]], 1) for n in range(SLOTS)], 0
    )
    scores = jnp.dot(keys, queries, preferred_element_type=jnp.float32)
    count = live_counts(couple, counts)
    top = None
    for n in range(SLOTS):
        tile = scores[n * BLK : (n + 1) * BLK]
        if n == 0:
            tile = jnp.where(key_row <= query_row, tile, LOW)
            top = tile.reshape(16, 8, PAIR).max(0)
        else:
            best = tile.reshape(16, 8, PAIR).max(0)
            top = jnp.maximum(top, jnp.where(n < count, best, LOW))
        score_ref[n * BLK : (n + 1) * BLK, :] = tile
    top_ref[...] = jnp.max(top, axis=0, keepdims=True)


def live_counts(couple, counts):
    lane = lax.broadcasted_iota(jnp.int32, (1, PAIR), 1)
    return jnp.where(lane < BLK, counts[2 * couple], counts[2 * couple + 1])


def weigh_couple(couple, counts, score_ref, top_ref):
    count = live_counts(couple, counts)
    top = top_ref[...]
    total = jnp.zeros((8, PAIR), jnp.float32)
    tiles = []
    for n in range(SLOTS):
        shift = top if n == 0 else jnp.where(n < count, top, -LOW)
        weights = jnp.exp2((score_ref[n * BLK : (n + 1) * BLK, :] - shift) * EXP2_SCALE)
        total += weights.reshape(16, 8, PAIR).sum(0)
        tiles.append(weights.astype(jnp.bfloat16))
    return tiles, jnp.sum(total, axis=0, keepdims=True)


def combine_couple(couple, weights, total, lists, values, out_ref):
    head = 2 * (couple % SIDE_COUPLES)
    for half in range(2):
        pair = 2 * couple + half
        tiles = cat([values[lists[pair * SLOTS + n]] for n in range(SLOTS)], 1)
        lanes = slice(half * BLK, (half + 1) * BLK)
        summed = jnp.dot(tiles, weights[:, lanes], preferred_element_type=jnp.float32)
        attended = (summed / total[:, lanes]).T.astype(jnp.bfloat16)
        cols = pl.ds(pl.multiple_of((head + half) * BLK, BLK), BLK)
        out_ref[:, cols] = attended


def pipelined(first, score, weigh, buffers, rest):
    score_a, top_a, score_b, top_b = buffers
    score(first, score_a, top_a)
    for copy in rest:
        copy.wait()

    last = first + SIDE_COUPLES - 1

    def step(index, carry):
        couple = first + 2 * index
        score(couple + 1, score_b, top_b)
        weigh(couple, score_a, top_a)
        score(jnp.minimum(couple + 2, last), score_a, top_a)
        weigh(couple + 1, score_b, top_b)
        return carry

    lax.fori_loop(0, SIDE_COUPLES // 2, step, 0)


BUFFERS = [pltpu.VMEM((SPAN, PAIR), jnp.float32), pltpu.VMEM((1, PAIR), jnp.float32)] * 2


def hold_kernel(source_ref, after_ref, out_ref, sem):
    copy = pltpu.make_async_copy(source_ref, out_ref, sem)
    copy.start()
    copy.wait()


def hold_call(source, after):
    return pl.pallas_call(
        hold_kernel,
        name="hold_weight",
        in_specs=[HBM, HBM],
        out_specs=VMEM,
        out_shape=pltpu.VMEM(source.shape, source.dtype),
        scratch_shapes=[pltpu.SemaphoreType.DMA],
        compiler_params=pltpu.CompilerParams(vmem_limit_bytes=4 * MIB),
    )(stay(source), after)


def prepare_kernel(key_ref, value_ref, mine_ref, theirs_ref, key_held, value_held, sems):
    core = lax.rem(lax.axis_index("seq"), CORES)
    copies = [
        pltpu.make_async_copy(key_ref, key_held, sems.at[0]),
        pltpu.make_async_copy(value_ref, value_held, sems.at[1]),
    ]
    for copy in copies:
        copy.start()
    for copy in copies:
        copy.wait()
    for out_ref, head in ((mine_ref, core), (theirs_ref, 1 - core)):
        for block in range(out_ref.shape[1]):
            rows = slice(block * BLK, (block + 1) * BLK)
            out_ref[0, block] = key_held[head, rows, :]
            out_ref[1, block] = value_held[head, rows, :].T


def prepare_call(keys, values):
    blocks = keys.shape[1] // BLK
    shape = jax.ShapeDtypeStruct((2, blocks, BLK, BLK), jnp.bfloat16)
    return pl.pallas_call(
        prepare_kernel,
        name="prepare",
        in_specs=[HBM] * 2,
        out_specs=[VMEM] * 2,
        out_shape=[shape, shape],
        scratch_shapes=[pltpu.VMEM(keys.shape, keys.dtype)] * 2
        + [pltpu.SemaphoreType.DMA((2,))],
        compiler_params=pltpu.CompilerParams(vmem_limit_bytes=6 * MIB),
        cost_estimate=SHORT,
    )(stay(keys), stay(values))


def bring(pieces, tables, sems, places):
    copies = []
    for index, (piece, (table, at)) in enumerate(zip(pieces, places)):
        copies.append(
            pltpu.make_async_copy(
                piece, tables[table].at[pl.ds(at, piece.shape[0])], sems.at[index]
            )
        )
    for copy in copies:
        copy.start()
    return copies


def tables_kernel(places, *refs):
    pieces, tables, sems = refs[: len(places)], refs[len(places) : -1], refs[-1]
    for copy in bring(pieces, tables, sems, places):
        copy.wait()


def tables_call(places, pieces):
    return pl.pallas_call(
        functools.partial(tables_kernel, places),
        name="tables",
        in_specs=[HBM] * len(pieces),
        out_specs=[VMEM] * 2,
        out_shape=[pltpu.VMEM((BLK, BLK, BLK), jnp.bfloat16)] * 2,
        scratch_shapes=[pltpu.SemaphoreType.DMA((len(pieces),))],
        compiler_params=pltpu.CompilerParams(vmem_limit_bytes=4 * MIB),
        cost_estimate=SHORT,
    )(*map(stay, pieces))


def attend_kernel(first, places, lists, counts, place, q_ref, after_ref, also_ref, *refs):
    if places:
        pieces, refs = refs[: len(places)], refs[len(places) + 2 :]
        out_ref, keys, values, *buffers, sems = refs
        copies = bring(pieces, (keys, values), sems, places)
        copies[0].wait()
        rest = copies[1:]
    else:
        keys, values, out_ref, *buffers = refs
        rest = []

    def score(couple, score_ref, top_ref):
        score_couple(couple, lists, counts, place, q_ref, keys, score_ref, top_ref)

    def weigh(couple, score_ref, top_ref):
        tiles, total = weigh_couple(couple, counts, score_ref, top_ref)
        combine_couple(couple, cat(tiles, 0), total, lists, values, out_ref)

    pipelined(first, score, weigh, buffers, rest)


def attend_call(
    name, chunk, side, lists, counts, place, queries, after, tables, pieces=(), places=(), cost=SHORT
):
    out_shape = [jax.ShapeDtypeStruct((BLK, 8 * BLK), jnp.bfloat16)]
    scratch = list(BUFFERS)
    aliases = {}
    if pieces:
        out_shape += [pltpu.VMEM(table.shape, table.dtype) for table in tables]
        scratch += [pltpu.SemaphoreType.DMA((len(pieces),))]
        aliases = {6 + len(pieces): 1, 7 + len(pieces): 2}
    return pl.pallas_call(
        functools.partial(attend_kernel, chunk * CHUNK_COUPLES + side * SIDE_COUPLES, places),
        name=name,
        grid_spec=pltpu.PrefetchScalarGridSpec(
            num_scalar_prefetch=3,
            grid=(1,),
            in_specs=[VMEM] + [VMEM if pieces else HBM] * 2 + [HBM] * len(pieces) + [VMEM] * len(tables),
            out_specs=[VMEM] * len(out_shape),
            scratch_shapes=scratch,
        ),
        out_shape=out_shape,
        input_output_aliases=aliases,
        compiler_params=pltpu.CompilerParams(vmem_limit_bytes=10 * MIB),
        cost_estimate=cost,
    )(lists, counts, place, queries, *after, *map(stay, pieces), *tables)


def queries_kernel(place, source_ref, after_ref, mine_ref, theirs_ref, sems):
    heads = mine_ref.shape[0]
    core = place[0]
    copies = [
        pltpu.make_async_copy(
            source_ref.at[pl.ds(owner * heads, heads)], out_ref, sems.at[index]
        )
        for index, (owner, out_ref) in enumerate(((core, mine_ref), (1 - core, theirs_ref)))
    ]
    for copy in copies:
        copy.start()
    for copy in copies:
        copy.wait()


def queries_call(place, queries, heads, after):
    shape = jax.ShapeDtypeStruct((heads,) + queries.shape[1:], queries.dtype)
    return pl.pallas_call(
        queries_kernel,
        name="queries",
        grid_spec=pltpu.PrefetchScalarGridSpec(
            num_scalar_prefetch=1,
            grid=(1,),
            in_specs=[HBM, HBM],
            out_specs=[VMEM, VMEM],
            scratch_shapes=[pltpu.SemaphoreType.DMA((2,))],
        ),
        out_shape=[shape, shape],
        compiler_params=pltpu.CompilerParams(vmem_limit_bytes=8 * MIB),
        cost_estimate=SHORT,
    )(place, stay(queries), after)


def project_kernel(kind, place, mine_ref, theirs_ref, held_ref, after_ref, *refs):
    out_ref = refs[-1]
    width = held_ref.shape[1]
    tile = 1024
    core = place[0]
    mine = mine_ref[...]
    theirs = theirs_ref[...]
    both = cat([jnp.where(core == 0, mine, theirs), jnp.where(core == 0, theirs, mine)], 1)
    for at in range(0, width, tile):
        cols = slice(at, at + tile)
        total = jnp.dot(both, held_ref[:, cols], preferred_element_type=jnp.float32)
        if kind in ("last", "own"):
            total = total + refs[0][:, cols].astype(jnp.float32)
        out_ref[:, cols] = total.astype(out_ref.dtype)


def project_call(kind, place, mine, theirs, held, after, *arrived):
    width = held.shape[1]
    out_type = jnp.float32 if kind == "own" else jnp.bfloat16
    return pl.pallas_call(
        functools.partial(project_kernel, kind),
        name="project_" + kind,
        grid_spec=pltpu.PrefetchScalarGridSpec(
            num_scalar_prefetch=1,
            grid=(1,),
            in_specs=[VMEM] * 3 + [HBM] + [VMEM] * len(arrived),
            out_specs=VMEM,
        ),
        out_shape=jax.ShapeDtypeStruct((BLK, width), out_type),
        compiler_params=pltpu.CompilerParams(vmem_limit_bytes=8 * MIB),
        cost_estimate=MIDDLE if kind == "own" else SHORT,
    )(place, mine, theirs, held, after, *arrived)


def chip_perm(phase, step):
    pairs = []
    for z in range(RING):
        for y in range(RING):
            for core in range(CORES):
                if (core == 0) == (phase == 0):
                    to_z, to_y = z, (y + step) % RING
                else:
                    to_z, to_y = (z + step) % RING, y
                pairs.append(((z * RING + y) * CORES + core, (to_z * RING + to_y) * CORES + core))
    return pairs


SWAP = [(i, i ^ 1) for i in range(SEQ_DEVICES)]


def along(array, phase, step):
    return lax.ppermute(array, "seq", chip_perm(phase, step))


def swap(array):
    return lax.ppermute(array, "seq", SWAP)


def turn(array, step):
    pairs = []
    for seq in range(SEQ_DEVICES):
        way = step if seq % CORES == 0 else -step
        pairs += [(seq * RING + i, seq * RING + (i + way) % RING) for i in range(RING)]
    return lax.ppermute(array, ("seq", "grp"), pairs)


def gather_tiles(own):
    parts = [own, along(own, 0, 1), along(own, 0, -1), along(own, 0, 2)]
    keys = cat([part[0] for part in parts], 0)
    values = cat([part[1] for part in parts], 0)
    keys_left, values_right = along(keys, 1, 1), along(values, 1, -1)
    values_left, keys_right = along(values, 1, 1), along(keys, 1, -1)
    keys_far, values_far = along(keys_left, 1, 1), along(values_right, 1, -1)
    size = keys.shape[0]
    early = [keys, keys_left, keys_right, values, values_left, values_right]
    early_places = ((0, 0), (0, size), (0, 2 * size), (1, 0), (1, size), (1, 2 * size))
    late = [keys_far, values_far]
    late_places = ((0, 3 * size), (1, 3 * size))
    return parts[1], early, early_places, late, late_places


def body(query_states, key_states, value_states, tile_keys, tile_count, out_weight):
    head_group, row_count, width = query_states.shape
    kv_group = key_states.shape[0]
    blocks = row_count // BLK
    heads = head_group // kv_group
    seq_place = lax.axis_index("seq")
    grp_place = lax.axis_index("grp")
    core = seq_place % CORES
    chip = seq_place // CORES
    chip_z, chip_y = chip // RING, chip % RING

    ways = jnp.array([[2, 3, 1, 0], [2, 1, 3, 0]], jnp.int32)
    mine_chunks = jnp.where(core == 0, ways[0], ways[1])
    theirs_chunks = jnp.where(core == 0, ways[1], ways[0])
    chunks = (grp_place + jnp.stack([theirs_chunks, mine_chunks])) % RING
    place = jnp.concatenate([core[None], chunks.reshape(-1)]).astype(jnp.int32)
    mine, theirs = prepare_call(key_states, value_states)
    neighbor, early, early_places, late, late_places = gather_tiles(cat([mine, swap(theirs)], 1))

    queries_mine, queries_theirs = queries_call(place, query_states, heads, neighbor)
    queries = jnp.stack([swap(queries_theirs), queries_mine])

    sides = jnp.stack([1 - core, core])
    order = (chip * 2 * blocks + sides[None, :] * blocks + chunks.T).reshape(-1)
    my_lists = lax.dynamic_slice_in_dim(tile_keys, core * heads, heads, 0)
    my_counts = lax.dynamic_slice_in_dim(tile_count, core * heads, heads, 0)
    lists = jnp.swapaxes(jnp.take(my_lists, order, axis=1), 0, 1)
    counts = jnp.swapaxes(jnp.take(my_counts, order, axis=1), 0, 1).reshape(-1)

    span = 2 * blocks
    from_chip = lists // span
    inside = lists % span
    step_z = (from_chip // RING - chip_z) % RING
    step_y = (from_chip % RING - chip_y) % RING

    def arrival(step):
        return jnp.where(step == 1, 2, jnp.where(step == 2, 3, jnp.where(step == 3, 1, 0)))

    inner = arrival(jnp.where(core == 0, step_y, step_z))
    outer = arrival(jnp.where(core == 0, step_z, step_y))
    lists = (
        (outer * RING + inner) * span
        + (inside // blocks + core) % CORES * blocks
        + inside % blocks
    ).reshape(-1)

    held = hold_call(out_weight, neighbor)

    tables = tables_call(early_places, early)
    far_theirs, *tables = attend_call(
        "far_theirs", 0, 0, lists, counts, place, queries, (held, held), tables, late, late_places
    )

    def attend(name, chunk, side, after, cost=SHORT):
        (out,) = attend_call(
            name, chunk, side, lists, counts, place, queries, after, tables, cost=cost
        )
        return out

    far_mine = attend("far_mine", 0, 1, (far_theirs, far_theirs))
    far = project_call("far", place, far_mine, swap(far_theirs), held, far_mine)
    passed = turn(far, 1)
    near_theirs = attend("near_theirs", 1, 0, (far, far))
    near_mine = attend("near_mine", 1, 1, (near_theirs, near_theirs))
    near = project_call("near", place, near_mine, swap(near_theirs), held, near_mine)
    arrived = turn(near, -1)
    last_theirs = attend("last_theirs", 2, 0, (near, near))
    last_mine = attend("last_mine", 2, 1, (last_theirs, last_theirs))
    last = project_call("last", place, last_mine, swap(last_theirs), held, last_mine, passed)
    arrived_last = turn(last, 1)
    own_theirs = attend("own_theirs", 3, 0, (last, arrived))
    own_mine = attend("own_mine", 3, 1, (own_theirs, own_theirs))
    own = project_call("own", place, own_mine, swap(own_theirs), held, own_mine, arrived)
    total = own + arrived_last.astype(jnp.float32)
    return total.astype(jnp.bfloat16)


def solution(mesh):
    placed = (
        P("grp", "seq", None),
        P("grp", "seq", None),
        P("grp", "seq", None),
        P("grp", None, None),
        P("grp", None),
        P("grp", None),
    )
    return jax.shard_map(
        body, mesh=mesh, in_specs=placed, out_specs=P(("seq", "grp"), None), check_vma=False
    )
```

```python
import functools
import math

import jax
import jax.numpy as jnp
from jax import lax
from jax.experimental import pallas as pl
from jax.experimental.pallas import tpu as pltpu
from jax.sharding import PartitionSpec as P

BLK = 128
SLOTS = 16
PAIR = 2 * BLK
SPAN = SLOTS * BLK
RING = 4
CORES = 2
SEQ_DEVICES = RING * RING * CORES
SIDE_COUPLES = 4
PEELED = ("near_theirs", "near_mine", "last_theirs", "last_mine")
CHUNK_COUPLES = 2 * SIDE_COUPLES
EXP2_SCALE = float(BLK ** -0.5 * math.log2(math.e))
LOW = -1e30
MIB = 2**20

SHORT = pl.CostEstimate(flops=1, bytes_accessed=1, transcendentals=0)
MIDDLE = pl.CostEstimate(flops=2 * 10**9, bytes_accessed=10**7, transcendentals=0)

VMEM = pl.BlockSpec(memory_space=pltpu.VMEM)
HBM = pl.BlockSpec(memory_space=pltpu.HBM)


def stay(array):
    return pltpu.with_memory_space_constraint(array, pltpu.HBM)


def cat(parts, axis):
    return jnp.concatenate(parts, axis)


def score_couple(couple, lists, counts, place, q_ref, table, score_ref, top_ref):
    key_row = lax.broadcasted_iota(jnp.int32, (BLK, PAIR), 0)
    query_row = lax.broadcasted_iota(jnp.int32, (BLK, PAIR), 1) % BLK
    zero = jnp.zeros((BLK, BLK), jnp.bfloat16)
    chunk = couple // CHUNK_COUPLES
    side = couple // SIDE_COUPLES % 2
    head = 2 * (couple % SIDE_COUPLES)
    rows = pl.ds(pl.multiple_of(place[1 + side * RING + chunk] * BLK, BLK), BLK)
    qa = q_ref[side, head, rows, :].T
    qb = q_ref[side, head + 1, rows, :].T
    queries = cat([cat([qa, zero], 1), cat([zero, qb], 1)], 0)
    a = 2 * couple * SLOTS
    keys = cat(
        [cat([table[lists[a + n]], table[lists[a + SLOTS + n]]], 1) for n in range(SLOTS)], 0
    )
    scores = jnp.dot(keys, queries, preferred_element_type=jnp.float32)
    count = live_counts(couple, counts)
    top = None
    for n in range(SLOTS):
        tile = scores[n * BLK : (n + 1) * BLK]
        if n == 0:
            tile = jnp.where(key_row <= query_row, tile, LOW)
            top = tile.reshape(16, 8, PAIR).max(0)
        else:
            best = tile.reshape(16, 8, PAIR).max(0)
            top = jnp.maximum(top, jnp.where(n < count, best, LOW))
        score_ref[n * BLK : (n + 1) * BLK, :] = tile
    top_ref[...] = jnp.max(top, axis=0, keepdims=True)


def live_counts(couple, counts):
    lane = lax.broadcasted_iota(jnp.int32, (1, PAIR), 1)
    return jnp.where(lane < BLK, counts[2 * couple], counts[2 * couple + 1])


def weigh_couple(couple, counts, score_ref, top_ref):
    count = live_counts(couple, counts)
    top = top_ref[...]
    total = jnp.zeros((8, PAIR), jnp.float32)
    tiles = []
    for n in range(SLOTS):
        shift = top if n == 0 else jnp.where(n < count, top, -LOW)
        weights = jnp.exp2((score_ref[n * BLK : (n + 1) * BLK, :] - shift) * EXP2_SCALE)
        total += weights.reshape(16, 8, PAIR).sum(0)
        tiles.append(weights.astype(jnp.bfloat16))
    return tiles, jnp.sum(total, axis=0, keepdims=True)


def combine_couple(couple, weights, total, lists, values, out_ref):
    head = 2 * (couple % SIDE_COUPLES)
    for half in range(2):
        pair = 2 * couple + half
        tiles = cat([values[lists[pair * SLOTS + n]] for n in range(SLOTS)], 1)
        lanes = slice(half * BLK, (half + 1) * BLK)
        summed = jnp.dot(tiles, weights[:, lanes], preferred_element_type=jnp.float32)
        attended = (summed / total[:, lanes]).T.astype(jnp.bfloat16)
        cols = pl.ds(pl.multiple_of((head + half) * BLK, BLK), BLK)
        out_ref[:, cols] = attended


def pipelined(first, peel, score, weigh, buffers, rest):
    score_a, top_a, score_b, top_b = buffers
    score(first, score_a, top_a)
    for copy in rest:
        copy.wait()

    last = first + SIDE_COUPLES - 1

    def step(index, carry):
        couple = first + 2 * index
        score(couple + 1, score_b, top_b)
        weigh(couple, score_a, top_a)
        score(jnp.minimum(couple + 2, last), score_a, top_a)
        weigh(couple + 1, score_b, top_b)
        return carry

    if peel:
        step(0, 0)
        score(last, score_b, top_b)
        weigh(last - 1, score_a, top_a)
        weigh(last, score_b, top_b)
    else:
        lax.fori_loop(0, SIDE_COUPLES // 2, step, 0)


BUFFERS = [pltpu.VMEM((SPAN, PAIR), jnp.float32), pltpu.VMEM((1, PAIR), jnp.float32)] * 2


def hold_kernel(source_ref, after_ref, out_ref, sem):
    copy = pltpu.make_async_copy(source_ref, out_ref, sem)
    copy.start()
    copy.wait()


def hold_call(source, after):
    return pl.pallas_call(
        hold_kernel,
        name="hold_weight",
        in_specs=[HBM, HBM],
        out_specs=VMEM,
        out_shape=pltpu.VMEM(source.shape, source.dtype),
        scratch_shapes=[pltpu.SemaphoreType.DMA],
        compiler_params=pltpu.CompilerParams(vmem_limit_bytes=4 * MIB),
    )(stay(source), after)


def prepare_kernel(key_ref, value_ref, mine_ref, theirs_ref, key_held, value_held, sems):
    core = lax.rem(lax.axis_index("seq"), CORES)
    copies = [
        pltpu.make_async_copy(key_ref, key_held, sems.at[0]),
        pltpu.make_async_copy(value_ref, value_held, sems.at[1]),
    ]
    for copy in copies:
        copy.start()
    for copy in copies:
        copy.wait()
    for out_ref, head in ((mine_ref, core), (theirs_ref, 1 - core)):
        for block in range(out_ref.shape[1]):
            rows = slice(block * BLK, (block + 1) * BLK)
            out_ref[0, block] = key_held[head, rows, :]
            out_ref[1, block] = value_held[head, rows, :].T


def prepare_call(keys, values):
    blocks = keys.shape[1] // BLK
    shape = jax.ShapeDtypeStruct((2, blocks, BLK, BLK), jnp.bfloat16)
    return pl.pallas_call(
        prepare_kernel,
        name="prepare",
        in_specs=[HBM] * 2,
        out_specs=[VMEM] * 2,
        out_shape=[shape, shape],
        scratch_shapes=[pltpu.VMEM(keys.shape, keys.dtype)] * 2
        + [pltpu.SemaphoreType.DMA((2,))],
        compiler_params=pltpu.CompilerParams(vmem_limit_bytes=6 * MIB),
        cost_estimate=SHORT,
    )(stay(keys), stay(values))


def bring(pieces, tables, sems, places):
    copies = []
    for index, (piece, (table, at)) in enumerate(zip(pieces, places)):
        copies.append(
            pltpu.make_async_copy(
                piece, tables[table].at[pl.ds(at, piece.shape[0])], sems.at[index]
            )
        )
    for copy in copies:
        copy.start()
    return copies


def tables_kernel(places, *refs):
    pieces, tables, sems = refs[: len(places)], refs[len(places) : -1], refs[-1]
    for copy in bring(pieces, tables, sems, places):
        copy.wait()


def tables_call(places, pieces):
    return pl.pallas_call(
        functools.partial(tables_kernel, places),
        name="tables",
        in_specs=[HBM] * len(pieces),
        out_specs=[VMEM] * 2,
        out_shape=[pltpu.VMEM((BLK, BLK, BLK), jnp.bfloat16)] * 2,
        scratch_shapes=[pltpu.SemaphoreType.DMA((len(pieces),))],
        compiler_params=pltpu.CompilerParams(vmem_limit_bytes=4 * MIB),
        cost_estimate=SHORT,
    )(*map(stay, pieces))


def attend_kernel(name, first, places, lists, counts, place, q_ref, after_ref, also_ref, *refs):
    if places:
        pieces, refs = refs[: len(places)], refs[len(places) + 2 :]
        out_ref, keys, values, *buffers, sems = refs
        copies = bring(pieces, (keys, values), sems, places)
        copies[0].wait()
        rest = copies[1:]
    else:
        keys, values, out_ref, *buffers = refs
        rest = []

    def score(couple, score_ref, top_ref):
        score_couple(couple, lists, counts, place, q_ref, keys, score_ref, top_ref)

    def weigh(couple, score_ref, top_ref):
        tiles, total = weigh_couple(couple, counts, score_ref, top_ref)
        combine_couple(couple, cat(tiles, 0), total, lists, values, out_ref)

    pipelined(first, name in PEELED, score, weigh, buffers, rest)


def attend_call(
    name, chunk, side, lists, counts, place, queries, after, tables, pieces=(), places=(), cost=SHORT
):
    out_shape = [jax.ShapeDtypeStruct((BLK, 8 * BLK), jnp.bfloat16)]
    scratch = list(BUFFERS)
    aliases = {}
    if pieces:
        out_shape += [pltpu.VMEM(table.shape, table.dtype) for table in tables]
        scratch += [pltpu.SemaphoreType.DMA((len(pieces),))]
        aliases = {6 + len(pieces): 1, 7 + len(pieces): 2}
    return pl.pallas_call(
        functools.partial(attend_kernel, name, chunk * CHUNK_COUPLES + side * SIDE_COUPLES, places),
        name=name,
        grid_spec=pltpu.PrefetchScalarGridSpec(
            num_scalar_prefetch=3,
            grid=(1,),
            in_specs=[VMEM] + [VMEM if pieces else HBM] * 2 + [HBM] * len(pieces) + [VMEM] * len(tables),
            out_specs=[VMEM] * len(out_shape),
            scratch_shapes=scratch,
        ),
        out_shape=out_shape,
        input_output_aliases=aliases,
        compiler_params=pltpu.CompilerParams(vmem_limit_bytes=10 * MIB),
        cost_estimate=cost,
    )(lists, counts, place, queries, *after, *map(stay, pieces), *tables)


def queries_kernel(place, source_ref, after_ref, mine_ref, theirs_ref, sems):
    heads = mine_ref.shape[0]
    core = place[0]
    copies = [
        pltpu.make_async_copy(
            source_ref.at[pl.ds(owner * heads, heads)], out_ref, sems.at[index]
        )
        for index, (owner, out_ref) in enumerate(((core, mine_ref), (1 - core, theirs_ref)))
    ]
    for copy in copies:
        copy.start()
    for copy in copies:
        copy.wait()


def queries_call(place, queries, heads, after):
    shape = jax.ShapeDtypeStruct((heads,) + queries.shape[1:], queries.dtype)
    return pl.pallas_call(
        queries_kernel,
        name="queries",
        grid_spec=pltpu.PrefetchScalarGridSpec(
            num_scalar_prefetch=1,
            grid=(1,),
            in_specs=[HBM, HBM],
            out_specs=[VMEM, VMEM],
            scratch_shapes=[pltpu.SemaphoreType.DMA((2,))],
        ),
        out_shape=[shape, shape],
        compiler_params=pltpu.CompilerParams(vmem_limit_bytes=8 * MIB),
        cost_estimate=SHORT,
    )(place, stay(queries), after)


def project_kernel(kind, place, mine_ref, theirs_ref, held_ref, after_ref, *refs):
    out_ref = refs[-1]
    width = held_ref.shape[1]
    tile = 2048
    core = place[0]
    mine = mine_ref[...]
    theirs = theirs_ref[...]
    both = cat([jnp.where(core == 0, mine, theirs), jnp.where(core == 0, theirs, mine)], 1)

    def step(index, carry):
        cols = pl.ds(pl.multiple_of(index * tile, tile), tile)
        total = jnp.dot(both, held_ref[:, cols], preferred_element_type=jnp.float32)
        if kind in ("last", "own"):
            total = total + refs[0][:, cols].astype(jnp.float32)
        out_ref[:, cols] = total.astype(out_ref.dtype)
        return carry

    lax.fori_loop(0, width // tile, step, 0)


def project_call(kind, place, mine, theirs, held, after, *arrived):
    width = held.shape[1]
    out_type = jnp.float32 if kind == "own" else jnp.bfloat16
    return pl.pallas_call(
        functools.partial(project_kernel, kind),
        name="project_" + kind,
        grid_spec=pltpu.PrefetchScalarGridSpec(
            num_scalar_prefetch=1,
            grid=(1,),
            in_specs=[VMEM] * 3 + [HBM] + [VMEM] * len(arrived),
            out_specs=VMEM,
        ),
        out_shape=jax.ShapeDtypeStruct((BLK, width), out_type),
        compiler_params=pltpu.CompilerParams(vmem_limit_bytes=8 * MIB),
        cost_estimate=MIDDLE if kind == "own" else SHORT,
    )(place, mine, theirs, held, after, *arrived)


def chip_perm(phase, step):
    pairs = []
    for z in range(RING):
        for y in range(RING):
            for core in range(CORES):
                if (core == 0) == (phase == 0):
                    to_z, to_y = z, (y + step) % RING
                else:
                    to_z, to_y = (z + step) % RING, y
                pairs.append(((z * RING + y) * CORES + core, (to_z * RING + to_y) * CORES + core))
    return pairs


SWAP = [(i, i ^ 1) for i in range(SEQ_DEVICES)]


def along(array, phase, step):
    return lax.ppermute(array, "seq", chip_perm(phase, step))


def swap(array):
    return lax.ppermute(array, "seq", SWAP)


def turn(array, step):
    pairs = []
    for seq in range(SEQ_DEVICES):
        way = step if seq % CORES == 0 else -step
        pairs += [(seq * RING + i, seq * RING + (i + way) % RING) for i in range(RING)]
    return lax.ppermute(array, ("seq", "grp"), pairs)


def gather_tiles(own):
    parts = [own, along(own, 0, 1), along(own, 0, -1), along(own, 0, 2)]
    keys = cat([part[0] for part in parts], 0)
    values = cat([part[1] for part in parts], 0)
    keys_left, values_right = along(keys, 1, 1), along(values, 1, -1)
    values_left, keys_right = along(values, 1, 1), along(keys, 1, -1)
    keys_far, values_far = along(keys_left, 1, 1), along(values_right, 1, -1)
    size = keys.shape[0]
    early = [keys, keys_left, keys_right, values, values_left, values_right]
    early_places = ((0, 0), (0, size), (0, 2 * size), (1, 0), (1, size), (1, 2 * size))
    late = [keys_far, values_far]
    late_places = ((0, 3 * size), (1, 3 * size))
    return parts[1], early, early_places, late, late_places


def body(query_states, key_states, value_states, tile_keys, tile_count, out_weight):
    head_group, row_count, width = query_states.shape
    kv_group = key_states.shape[0]
    blocks = row_count // BLK
    heads = head_group // kv_group
    seq_place = lax.axis_index("seq")
    grp_place = lax.axis_index("grp")
    core = seq_place % CORES
    chip = seq_place // CORES
    chip_z, chip_y = chip // RING, chip % RING

    ways = jnp.array([[2, 3, 1, 0], [2, 1, 3, 0]], jnp.int32)
    mine_chunks = jnp.where(core == 0, ways[0], ways[1])
    theirs_chunks = jnp.where(core == 0, ways[1], ways[0])
    chunks = (grp_place + jnp.stack([theirs_chunks, mine_chunks])) % RING
    place = jnp.concatenate([core[None], chunks.reshape(-1)]).astype(jnp.int32)
    mine, theirs = prepare_call(key_states, value_states)
    neighbor, early, early_places, late, late_places = gather_tiles(cat([mine, swap(theirs)], 1))

    queries_mine, queries_theirs = queries_call(place, query_states, heads, neighbor)
    queries = jnp.stack([swap(queries_theirs), queries_mine])

    sides = jnp.stack([1 - core, core])
    order = (chip * 2 * blocks + sides[None, :] * blocks + chunks.T).reshape(-1)
    my_lists = lax.dynamic_slice_in_dim(tile_keys, core * heads, heads, 0)
    my_counts = lax.dynamic_slice_in_dim(tile_count, core * heads, heads, 0)
    lists = jnp.swapaxes(jnp.take(my_lists, order, axis=1), 0, 1)
    counts = jnp.swapaxes(jnp.take(my_counts, order, axis=1), 0, 1).reshape(-1)

    span = 2 * blocks
    from_chip = lists // span
    inside = lists % span
    step_z = (from_chip // RING - chip_z) % RING
    step_y = (from_chip % RING - chip_y) % RING

    def arrival(step):
        return jnp.where(step == 1, 2, jnp.where(step == 2, 3, jnp.where(step == 3, 1, 0)))

    inner = arrival(jnp.where(core == 0, step_y, step_z))
    outer = arrival(jnp.where(core == 0, step_z, step_y))
    lists = (
        (outer * RING + inner) * span
        + (inside // blocks + core) % CORES * blocks
        + inside % blocks
    ).reshape(-1)

    held = hold_call(out_weight, neighbor)

    tables = tables_call(early_places, early)
    far_theirs, *tables = attend_call(
        "far_theirs", 0, 0, lists, counts, place, queries, (held, held), tables, late, late_places
    )

    def attend(name, chunk, side, after, cost=SHORT):
        (out,) = attend_call(
            name, chunk, side, lists, counts, place, queries, after, tables, cost=cost
        )
        return out

    far_mine = attend("far_mine", 0, 1, (far_theirs, far_theirs))
    far = project_call("far", place, far_mine, swap(far_theirs), held, far_mine)
    passed = turn(far, 1)
    near_theirs = attend("near_theirs", 1, 0, (far, far))
    near_mine = attend("near_mine", 1, 1, (near_theirs, near_theirs))
    near = project_call("near", place, near_mine, swap(near_theirs), held, near_mine)
    arrived = turn(near, -1)
    last_theirs = attend("last_theirs", 2, 0, (near, near))
    last_mine = attend("last_mine", 2, 1, (last_theirs, last_theirs))
    last = project_call("last", place, last_mine, swap(last_theirs), held, last_mine, passed)
    arrived_last = turn(last, 1)
    own_theirs = attend("own_theirs", 3, 0, (last, arrived))
    own_mine = attend("own_mine", 3, 1, (own_theirs, own_theirs))
    own = project_call("own", place, own_mine, swap(own_theirs), held, own_mine, arrived)
    total = own + arrived_last.astype(jnp.float32)
    return total.astype(jnp.bfloat16)


def solution(mesh):
    placed = (
        P("grp", "seq", None),
        P("grp", "seq", None),
        P("grp", "seq", None),
        P("grp", None, None),
        P("grp", None),
        P("grp", None),
    )
    return jax.shard_map(
        body, mesh=mesh, in_specs=placed, out_specs=P(("seq", "grp"), None), check_vma=False
    )
```
